128 devices in a mesh: batch: 64 (over z, y, x), head: 2 (over core).
Axes of the slice: x: 4, y: 4, z: 4, core: 2. Of those that a mesh axis runs over, the one named last changes fastest.
Arguments:
- q_nope: bfloat16 [4, 64, 16384], P(None, 'batch', 'head'), may hold values from -6 to 6
- q_rope: bfloat16 [4, 64, 8192], P(None, 'batch', 'head'), may hold values from -180 to 180
- up_key: bfloat16 [128, 128, 512], P('head'), may hold values from -0.5 to 0.5
- up_value: bfloat16 [128, 512, 128], P('head'), may hold values from -2 to 2
- pool_latent: bfloat16 [6144, 64, 512], P('batch'), may hold values from -6 to 6
- pool_rope: bfloat16 [6144, 4096], P('batch'), may hold values from -6 to 6
- new_latent: bfloat16 [4, 64, 512], P(None, 'batch'), may hold values from -6 to 6
- new_rope: bfloat16 [64, 256], P('batch'), may hold values from -7 to 7
- page_shard: int32 [64, 352, 1], P('batch'), may hold values from 0 to 63; in each aligned block of 176 rows (0 to 175, 176 to 351, ..., all dimensions but the last counted through in order) at most 5 rows name the same one
- page_slot: int32 [64, 352], P('batch'), may hold values from 0 to 95
Outputs:
- attended: bfloat16 [4, 64, 16384], P(None, 'batch', 'head')
The draws below stay inside these ranges and needn't reach their ends.
Inputs may be any that keep to these rules, and one draw needn't show every extreme that they name: `page_shard`: in each aligned block of 176 consecutive kept pages of a row, no context shard is named more than 5 times, a bound that some block reaches.
All inputs are finite; a program needn't handle non-finite values.
Results may differ from the reference program's by a relative error of at most 0.038.
Values may be sent and summed in bfloat16 or wider, within the bound.
No kernel may reach another device: no remote copies, remote signals or barrier semaphores. Data moves between devices by JAX's collectives and lax.ppermute only.
A program may use at most 192 MiB of HBM per device.

```python
import math
import jax
import jax.numpy as jnp
import numpy as np
from jax import lax

HEADS = 128
NOPE = 128
ROPE = 64
LATENT = 512
VDIM = 128
PAGE = 64
STEPS = 4
KEEP = 352
PG = 96
ROWS = 64
POOL = 6144
KB = 176
CAP = 5
N_BATCH = 64


def rope_seed(key):
    return jax.random.truncated_normal(key, -4.0, 4.0, (ROWS, STEPS, ROPE), jnp.float32)


def draw_new_rope(key, part):
    seed_rows = rope_seed(key)
    fresh_keys = seed_rows
    return fresh_keys.reshape(ROWS, STEPS * ROPE).astype(jnp.bfloat16)


def draw_q_rope(key, part):
    key = jax.random.fold_in(key, 7)
    first_key = jax.random.fold_in(key, 0)
    values = jax.random.truncated_normal(first_key, -4.0, 4.0, (STEPS, ROWS, HEADS, ROPE), jnp.float32)
    return values.reshape(STEPS, ROWS, HEADS * ROPE).astype(jnp.bfloat16)


def plant(entries, stream_key, smallest, high):
    index_at = [jax.random.randint(jax.random.fold_in(stream_key, axis), (), 0, length) for axis, length in enumerate(entries.shape)]
    longest = entries.shape.index(max(entries.shape))
    neighbour = index_at[:longest] + [(index_at[longest] + 1) % entries.shape[longest]] + index_at[longest + 1:]
    return entries.at[tuple(index_at)].set(smallest).at[tuple(neighbour)].set(high)


def steps_of(own_key, dims, cuts, low, largest):
    gain, own = 1.0, jax.random.fold_in(own_key, 6)
    for position, blocks in cuts:
        heights = jnp.exp(jax.random.uniform(jax.random.fold_in(own, position), (blocks,), jnp.float32, low / len(cuts), largest / len(cuts)))
        gain = gain * jnp.repeat(heights, dims[position] // blocks).reshape([-1 if axis == position else 1 for axis in range(len(dims))])
    return gain


def shared_out(key, own, number, rows, amount, top, most, skew):
    ranking = jax.random.permutation(key, amount)
    packed, common = load_shares(amount, rows * top, most, skew, True), load_shares(amount, rows * top, most, skew, False)
    places = jnp.arange(amount)

    def named(sizes, rotation):
        used = int((sizes > 0).sum())
        fixed = max(1, used // 4)
        passed = fixed + (places - fixed + rotation * (used - fixed)) % max(1, amount - fixed)
        return jnp.zeros((amount,), jnp.int32).at[ranking[jnp.where(places < fixed, places, passed)]].set(jnp.asarray(sizes, jnp.int32))

    sizes = jnp.where(number % 4 == 0, named(packed, number // 4), named(common, number - number // 4 - 1))
    mixed = jax.random.permutation(jax.random.fold_in(own, 3), amount)
    source_of, taker = mixed[0:amount // 2 * 2:2], mixed[1:amount // 2 * 2:2]
    room = jnp.minimum(sizes[source_of] - 1, most - sizes[taker]) // 2
    room = jnp.where((source_of == ranking[0]) | (taker == ranking[0]) | (sizes[taker] == 0), 0, jnp.maximum(room, 0))
    passed = jax.random.randint(jax.random.fold_in(own, 4), (amount // 2,), 0, 1 << 20) % (room + 1)
    sizes = sizes.at[source_of].add(-passed).at[taker].add(passed)
    labels = jnp.searchsorted(jnp.cumsum(sizes), jnp.arange(rows * top), side="right").astype(jnp.int32)
    table = labels.reshape(top, rows).T
    table = table[jax.random.permutation(jax.random.fold_in(own, 1), rows)]
    rotation = jax.random.randint(jax.random.fold_in(own, 2), (rows, 1), 0, top)
    return jnp.take_along_axis(table, (jnp.arange(top)[None, :] + rotation) % top, axis=1)


def load_shares(amount, total, most, skew, full):
    weights = [(1 << 20) // math.isqrt(rank ** skew) + 1 for rank in range(1, amount + 1)]
    largest = most if full else min(most, max(-(-total // amount), total * weights[0] // sum(weights)))
    least = 1 if total - largest >= amount - 1 else 0
    holding, spare = [largest] + [least] * (amount - 1), total - largest - least * (amount - 1)
    while spare > 0:
        movable = [i for i in range(1, amount) if holding[i] < largest] or [i for i in range(1, amount) if holding[i] < most]
        pool, remaining = sum([weights[i] for i in movable]), spare
        for i in movable:
            extra = min(most - holding[i], max(1, remaining * weights[i] // pool), spare)
            holding[i] = holding[i] + extra
            spare = spare - extra
    return np.array(holding)


def scatter_about(stream_key, shape, deviation, bound, pieces=(), kind=jnp.bfloat16):
    array = jax.random.normal(stream_key, shape, jnp.float32) * deviation
    if len(pieces) > 0:
        array = steps_of(stream_key, shape, pieces, -0.22, 0.18) * array
    return jnp.clip(array, min=-bound, max=bound).astype(kind)


def setup_inputs(seed: int = 0) -> dict:
    splits = jax.random.split(jax.random.key(seed), 11)
    q_nope = scatter_about(splits[0], (STEPS, ROWS, HEADS * NOPE), 1.0, 6.0, ((1, 64), (2, 2)))
    q_rope = draw_q_rope(jax.random.fold_in(splits[10], 71), 0)
    up_key = scatter_about(splits[2], (HEADS, NOPE, LATENT), NOPE ** -0.5, 0.5, ((0, 2),))
    up_value = scatter_about(splits[3], (HEADS, LATENT, VDIM), (max(1, LATENT // 64)) ** -0.5, 2.0, ((0, 2),))
    pool_latent = scatter_about(splits[4], (POOL, PAGE, LATENT), 1.0, 6.0, ((0, 64),))
    pool_rope = scatter_about(splits[5], (POOL, PAGE * ROPE), 1.0, 6.0, ((0, 64),))
    new_latent = scatter_about(splits[6], (STEPS, ROWS, LATENT), 1.0, 6.0, ((1, 64),))
    new_rope = draw_new_rope(jax.random.fold_in(splits[10], 71), 0)
    page_shard_keys = jax.random.split(jax.random.fold_in(splits[8], 1), ROWS * KEEP // KB)
    page_shard_turns = jax.random.permutation(jax.random.fold_in(splits[8], 3), ROWS * KEEP // KB)
    page_shard = jax.vmap(lambda own, number: shared_out(jax.random.fold_in(splits[8], 2), own, number, KB, N_BATCH, 1, CAP, 2))(page_shard_keys, page_shard_turns).reshape((ROWS, KEEP, 1))
    page_slot = plant(jax.random.randint(splits[9], (ROWS, KEEP), 0, PG), jax.random.fold_in(splits[9], 1), 0, PG - 1).astype(jnp.int32)
    return {"q_nope": q_nope, "q_rope": q_rope, "up_key": up_key, "up_value": up_value, "pool_latent": pool_latent, "pool_rope": pool_rope, "new_latent": new_latent, "new_rope": new_rope, "page_shard": page_shard, "page_slot": page_slot}


def one_row(inputs_row):
    q_lat, q_rot, page_index, fresh_lat, fresh_rope, up_value, pool_latent, pool_rope = inputs_row
    score_scale = 1.0 / math.sqrt(NOPE + ROPE)
    key_rows = pool_latent[page_index].reshape(KEEP * PAGE, LATENT)
    rope_rows = pool_rope[page_index].reshape(KEEP * PAGE, ROPE)
    query_two = q_lat.reshape(STEPS * HEADS, LATENT)
    rotated_two = q_rot.reshape(STEPS * HEADS, ROPE)
    scores = (jnp.dot(query_two, key_rows.T, preferred_element_type=jnp.float32) + jnp.dot(rotated_two, rope_rows.T, preferred_element_type=jnp.float32)) * score_scale
    fresh = (jnp.dot(query_two, fresh_lat.T, preferred_element_type=jnp.float32) + jnp.dot(rotated_two, fresh_rope.T, preferred_element_type=jnp.float32)) * score_scale
    step_of = jnp.arange(STEPS * HEADS, dtype=jnp.int32) // HEADS
    allowed = jnp.arange(STEPS, dtype=jnp.int32)[None, :] <= step_of[:, None]
    fresh = jnp.where(allowed, fresh, -jnp.inf)
    row_max = jnp.maximum(lax.optimization_barrier(jnp.max(scores, axis=1)), lax.optimization_barrier(jnp.max(fresh, axis=1)))
    weights = jnp.exp(scores - row_max[:, None])
    fresh_weights = jnp.exp(fresh - row_max[:, None])
    total = lax.optimization_barrier(jnp.sum(weights, axis=1)) + lax.optimization_barrier(jnp.sum(fresh_weights, axis=1))
    mixed = jnp.dot(weights.astype(jnp.bfloat16), key_rows, preferred_element_type=jnp.float32) + jnp.dot(fresh_weights.astype(jnp.bfloat16), fresh_lat, preferred_element_type=jnp.float32)
    latent_out = (mixed / total[:, None]).astype(jnp.bfloat16).reshape(STEPS, HEADS, LATENT)
    projected = jnp.einsum('shl,hlv->shv', latent_out.astype(jnp.float32), up_value.astype(jnp.float32))
    return projected.astype(jnp.bfloat16).reshape(STEPS, HEADS * VDIM)

def reference(q_nope, q_rope, up_key, up_value, pool_latent, pool_rope, new_latent, new_rope, page_shard, page_slot):
    absorbed = jnp.einsum('srhn,hnl->rshl', q_nope.reshape(STEPS, ROWS, HEADS, NOPE).astype(jnp.float32), up_key.astype(jnp.float32)).astype(jnp.bfloat16)
    rotated = q_rope.reshape(STEPS, ROWS, HEADS, ROPE).transpose(1, 0, 2, 3)
    fresh_lat = new_latent.transpose(1, 0, 2)
    fresh_rope = new_rope.reshape(ROWS, STEPS, ROPE)
    page_rows = (page_shard[:, :, 0] * PG + page_slot).astype(jnp.int32)

    def apply_row(items):
        q_lat, q_rot, page_index, row_lat, row_rope = items
        return one_row((q_lat, q_rot, page_index, row_lat, row_rope, up_value, pool_latent, pool_rope))
    result = lax.map(apply_row, (absorbed, rotated, page_rows, fresh_lat, fresh_rope))
    return result.transpose(1, 0, 2)
```

```python
import math

import jax
import jax.numpy as jnp
from jax import lax
from jax.experimental import pallas as pl
from jax.experimental.pallas import tpu as pltpu
from jax.sharding import PartitionSpec as P

MAX_PAGES = 10
NEG = -1e30
VMEM_BYTES = 48 * 1024 * 1024


def absorb_kernel(q_ref, up_ref, out_ref):
    rows, _, nope = q_ref.shape
    latent = up_ref.shape[2]
    q = q_ref[...].astype(jnp.float32).reshape(rows, 2, 8, nope)
    first = lax.broadcasted_iota(jnp.int32, (rows, 8, nope), 1) < 4
    halves = []
    for pair in range(2):
        part = q[:, pair]
        wide = jnp.concatenate(
            [jnp.where(first, part, 0.0), jnp.where(first, 0.0, part)], axis=2
        )
        wide = wide.reshape(rows * 8, 2 * nope).astype(jnp.bfloat16)
        weight = up_ref[2 * pair : 2 * pair + 2].reshape(2 * nope, latent)
        out = jnp.dot(wide, weight, preferred_element_type=jnp.float32)
        halves.append(out.reshape(rows, 8, latent))
    out_ref[...] = jnp.concatenate(halves, axis=1).astype(jnp.bfloat16)


def absorb(packed, up_key):
    rows = packed.shape[0]
    heads, nope, latent = up_key.shape
    groups = heads // 4
    return pl.pallas_call(
        absorb_kernel,
        out_shape=jax.ShapeDtypeStruct((rows, heads * 4, latent), jnp.bfloat16),
        grid=(groups,),
        in_specs=[
            pl.BlockSpec((rows, 16, nope), lambda j: (0, j, 0)),
            pl.BlockSpec((4, nope, latent), lambda j: (j, 0, 0)),
        ],
        out_specs=pl.BlockSpec((rows, 16, latent), lambda j: (0, j, 0)),
        compiler_params=pltpu.CompilerParams(vmem_limit_bytes=VMEM_BYTES),
        name="absorb",
    )(packed, up_key)


def attend_kernel(
    scale, counts_ref, slots_ref, q_ref, rope_ref, lat_ref, keyrope_ref, out_ref, lse_ref,
    keys, rotated
):
    r = pl.program_id(0)
    queries = q_ref.shape[1]
    latent = q_ref.shape[2]
    page = lat_ref.shape[1]
    count = counts_ref[r]

    def run(pages):
        tokens = pages * page
        for k in range(pages):
            slot = slots_ref[r, k]
            keys[k * page : (k + 1) * page, :] = lat_ref[slot]
            rotated[k * page : (k + 1) * page, :] = keyrope_ref[slot]
        key = keys[0:tokens, :]
        key_rope = rotated[0:tokens, :]
        packed = rope_ref[0]
        half = packed.shape[1] // 2
        q_rope = jnp.concatenate([packed[:, :half], packed[:, half:]], axis=0)
        nt = (((1,), (1,)), ((), ()))
        scores = lax.dot_general(q_ref[0], key, nt, preferred_element_type=jnp.float32)
        scores += lax.dot_general(q_rope, key_rope, nt, preferred_element_type=jnp.float32)
        scores *= scale
        token = lax.broadcasted_iota(jnp.int32, (queries, tokens), 1)
        scores = jnp.where(token < count * page, scores, NEG)
        top = jnp.max(scores, axis=1, keepdims=True)
        weights = jnp.exp(scores - top)
        total = jnp.sum(weights, axis=1, keepdims=True)
        mixed = jnp.dot(weights.astype(jnp.bfloat16), key, preferred_element_type=jnp.float32)
        out_ref[0] = (mixed / total).astype(jnp.bfloat16)
        lse = jnp.broadcast_to(top + jnp.log(total), (queries, 128))
        lse_ref[0] = lse.T[0:1, :]

    pl.when(count <= 4)(lambda: run(4))
    pl.when((count > 4) & (count <= 6))(lambda: run(6))
    pl.when((count > 6) & (count <= 8))(lambda: run(8))
    pl.when(count > 8)(lambda: run(10))


def attend(counts, slots, absorbed, packed, pool_latent, pool_rope, scale):
    rows, queries, latent = absorbed.shape
    slots_total, page, _ = pool_latent.shape
    rope = pool_rope.shape[2]
    grid_spec = pltpu.PrefetchScalarGridSpec(
        num_scalar_prefetch=2,
        grid=(rows,),
        in_specs=[
            pl.BlockSpec((1, queries, latent), lambda r, *_: (r, 0, 0)),
            pl.BlockSpec((1, queries // 2, 128), lambda r, *_: (r, 2, 0)),
            pl.BlockSpec((slots_total, page, latent), lambda r, *_: (0, 0, 0)),
            pl.BlockSpec((slots_total, page, rope), lambda r, *_: (0, 0, 0)),
        ],
        out_specs=[
            pl.BlockSpec((1, queries, latent), lambda r, *_: (r, 0, 0)),
            pl.BlockSpec((1, 1, queries), lambda r, *_: (r, 0, 0)),
        ],
        scratch_shapes=[
            pltpu.VMEM((MAX_PAGES * page, latent), jnp.bfloat16),
            pltpu.VMEM((MAX_PAGES * page, rope), jnp.bfloat16),
        ],
    )
    return pl.pallas_call(
        lambda *refs: attend_kernel(scale, *refs),
        out_shape=[
            jax.ShapeDtypeStruct((rows, queries, latent), jnp.bfloat16),
            jax.ShapeDtypeStruct((rows, 1, queries), jnp.float32),
        ],
        grid_spec=grid_spec,
        compiler_params=pltpu.CompilerParams(vmem_limit_bytes=VMEM_BYTES),
        name="attend",
    )(counts, slots, absorbed, packed, pool_latent, pool_rope)


def project_kernel(mixed_ref, up_ref, out_ref):
    rows, _, latent = mixed_ref.shape
    value = up_ref.shape[2]
    mixed = mixed_ref[...].astype(jnp.float32).reshape(rows, 2, 8, latent)
    first = lax.broadcasted_iota(jnp.int32, (rows, 8, value), 1) < 4
    halves = []
    for pair in range(2):
        part = mixed[:, pair].reshape(rows * 8, latent).astype(jnp.bfloat16)
        weight = jnp.concatenate([up_ref[2 * pair], up_ref[2 * pair + 1]], axis=1)
        out = jnp.dot(part, weight, preferred_element_type=jnp.float32)
        out = out.reshape(rows, 8, 2 * value)
        halves.append(jnp.where(first, out[:, :, :value], out[:, :, value:]))
    out_ref[...] = jnp.concatenate(halves, axis=1).astype(jnp.bfloat16)


def project(mixed, up_value):
    rows, queries, latent = mixed.shape
    heads, _, value = up_value.shape
    return pl.pallas_call(
        project_kernel,
        out_shape=jax.ShapeDtypeStruct((rows, queries, value), jnp.bfloat16),
        grid=(heads // 4,),
        in_specs=[
            pl.BlockSpec((rows, 16, latent), lambda j: (0, j, 0)),
            pl.BlockSpec((4, latent, value), lambda j: (j, 0, 0)),
        ],
        out_specs=pl.BlockSpec((rows, 16, value), lambda j: (0, j, 0)),
        compiler_params=pltpu.CompilerParams(vmem_limit_bytes=VMEM_BYTES),
        name="project",
    )(mixed, up_value)


def fresh_part(q_nope, q_rope, up_key, up_value, new_latent, new_rope, scale):
    steps, heads, _ = q_nope.shape
    latent = up_key.shape[2]
    absorbed = jnp.einsum(
        "shn,hnl->hsl", q_nope, up_key, preferred_element_type=jnp.float32
    ).astype(jnp.bfloat16)
    scores = (
        jnp.einsum("hsl,tl->hst", absorbed, new_latent, preferred_element_type=jnp.float32)
        + jnp.einsum("she,te->hst", q_rope, new_rope, preferred_element_type=jnp.float32)
    ) * scale
    at = jnp.arange(steps, dtype=jnp.int32)
    allowed = at[None, None, :] <= at[None, :, None]
    scores = jnp.where(allowed, scores, NEG)
    top = jnp.max(scores, axis=2, keepdims=True)
    weights = jnp.where(allowed, jnp.exp(scores - top), 0.0)
    total = jnp.sum(weights, axis=2, keepdims=True)
    mixed = jnp.einsum(
        "hst,tl->hsl", weights.astype(jnp.bfloat16), new_latent, preferred_element_type=jnp.float32
    )
    mixed = (mixed / total).astype(jnp.bfloat16)
    out = jnp.einsum("hsl,hlv->hsv", mixed, up_value, preferred_element_type=jnp.float32)
    return out, (top + jnp.log(total))[:, :, 0]


def page_lists(page_shard, page_slot, shards):
    kept = page_shard.shape[0]
    rank = jnp.sum(
        (page_shard[:, None] == page_shard[None, :])
        & (jnp.arange(kept)[None, :] < jnp.arange(kept)[:, None]),
        axis=1,
    )
    here = page_shard[None, :] == jnp.arange(shards, dtype=jnp.int32)[:, None]
    counts = jnp.sum(here, axis=1).astype(jnp.int32)
    at = jnp.arange(MAX_PAGES)[None, :, None]
    slots = jnp.sum(
        jnp.where(here[:, None, :] & (rank[None, None, :] == at), page_slot[None, None, :], 0),
        axis=2,
    ).astype(jnp.int32)
    return jnp.concatenate(
        [counts[:, None], slots, jnp.zeros((shards, 15 - MAX_PAGES), jnp.int32)], axis=1
    )


def exchange(x):
    return lax.all_to_all(x, "batch", split_axis=0, concat_axis=0, tiled=True)


def per_device(
    q_nope, q_rope, up_key, up_value, pool_latent, pool_rope,
    new_latent, new_rope, page_shard, page_slot
):
    shards = lax.axis_size("batch")
    steps = q_nope.shape[0]
    heads, nope, latent = up_key.shape
    value = up_value.shape[2]
    slots_total, page, _ = pool_latent.shape
    rope = pool_rope.shape[1] // page
    scale = 1.0 / math.sqrt(nope + rope)
    q_nope = q_nope.reshape(steps, heads, nope)
    q_rope = q_rope.reshape(steps, heads, rope)

    nope_rows = q_nope.transpose(1, 0, 2).reshape(heads * steps, nope)
    rope_rows = q_rope.transpose(1, 0, 2).reshape(2, heads * steps // 2, rope)
    rope_rows = rope_rows.transpose(1, 0, 2).reshape(heads * steps // 2, 2 * rope)
    own = jnp.concatenate([nope_rows, rope_rows], axis=0)
    packed = exchange(jnp.broadcast_to(own[None], (shards,) + own.shape))

    lists = exchange(page_lists(page_shard[0, :, 0], page_slot[0], shards))
    fresh_out, fresh_lse = fresh_part(
        q_nope, q_rope, up_key, up_value, new_latent[:, 0], new_rope.reshape(steps, rope), scale
    )
    pool_rope = pool_rope.reshape(slots_total, page, rope)

    absorbed = absorb(packed, up_key)
    mixed, lse = attend(
        lists[:, 0], lists[:, 1 : 1 + MAX_PAGES], absorbed, packed, pool_latent, pool_rope, scale
    )
    lse = exchange(lse[:, 0, :])
    parts = exchange(project(mixed, up_value))

    fresh_lse = fresh_lse.reshape(1, heads * steps)
    top = jnp.maximum(jnp.max(lse, axis=0, keepdims=True), fresh_lse)
    share = jnp.exp(lse - top)
    fresh_share = jnp.exp(fresh_lse - top)
    total = jnp.sum(share, axis=0, keepdims=True) + fresh_share
    share = share / total
    fresh_share = (fresh_share / total).reshape(heads * steps, 1)
    out = jnp.sum(parts.astype(jnp.float32) * share[:, :, None], axis=0)
    out = out + fresh_share * fresh_out.reshape(heads * steps, value)
    out = out.astype(jnp.bfloat16).reshape(heads, steps, value).transpose(1, 0, 2)
    return out.reshape(steps, 1, heads * value)


def solution(mesh):
    placed = (
        P(None, "batch", "head"),
        P(None, "batch", "head"),
        P("head", None, None),
        P("head", None, None),
        P("batch", None, None),
        P("batch", None),
        P(None, "batch", None),
        P("batch", None),
        P("batch", None, None),
        P("batch", None),
    )
    return jax.shard_map(
        per_device, mesh=mesh, in_specs=placed, out_specs=P(None, "batch", "head"), check_vma=False
    )
```

```python
import functools
import math

import jax
import jax.numpy as jnp
from jax import lax
from jax.experimental import pallas as pl
from jax.experimental.pallas import tpu as pltpu
from jax.sharding import PartitionSpec as P

MAX_PAGES = 10
NEG = -1e30
VMEM_BYTES = 62 * 1024 * 1024
PER = 2
PIECES = 4
NT = (((1,), (1,)), ((), ()))


def sixteen(at):
    return pl.ds(pl.multiple_of(at * 16, 16), 16)

def absorb_step(at, packed, up_ref, held):
    rows, _, nope = packed.shape
    latent = up_ref.shape[2]
    q = packed[:, sixteen(at), :].astype(jnp.float32).reshape(rows, 2, 8, nope)
    first = lax.broadcasted_iota(jnp.int32, (rows, 8, nope), 1) < 4
    halves = []
    for pair in range(2):
        part = q[:, pair]
        wide = jnp.concatenate([jnp.where(first, part, 0.0), jnp.where(first, 0.0, part)], axis=2)
        wide = wide.reshape(rows * 8, 2 * nope).astype(jnp.bfloat16)
        weight = up_ref[pl.ds(at * 4 + 2 * pair, 2)].reshape(2 * nope, latent)
        out = jnp.dot(wide, weight, preferred_element_type=jnp.float32)
        halves.append(out.reshape(rows, 8, latent))
    held[:, sixteen(at), :] = jnp.concatenate(halves, axis=1).astype(jnp.bfloat16)

def project_step(at, held, up_ref, packed):
    rows, _, latent = held.shape
    value = up_ref.shape[2]
    mixed = held[:, sixteen(at), :].astype(jnp.float32).reshape(rows, 2, 8, latent)
    first = lax.broadcasted_iota(jnp.int32, (rows, 8, value), 1) < 4
    halves = []
    for pair in range(2):
        part = mixed[:, pair].reshape(rows * 8, latent).astype(jnp.bfloat16)
        at_head = at * 4 + 2 * pair
        weight = jnp.concatenate([up_ref[at_head], up_ref[at_head + 1]], axis=1)
        out = jnp.dot(part, weight, preferred_element_type=jnp.float32)
        out = out.reshape(rows, 8, 2 * value)
        halves.append(jnp.where(first, out[:, :, :value], out[:, :, value:]))
    packed[:, sixteen(at), :] = jnp.concatenate(halves, axis=1).astype(jnp.bfloat16)

def attend_step(scale, at, counts_ref, slots_ref, packed_ref, lat_ref, keyrope_ref, held, keys, rotated, tops, totals):
    queries, latent = held.shape[1:]
    page = lat_ref.shape[1]
    counts = [counts_ref[at * PER + i] for i in range(PER)]
    most = functools.reduce(jnp.maximum, counts)

    def run(pages):
        tokens = pages * page
        lanes = lax.broadcasted_iota(jnp.int32, (queries, 128), 1)
        token = lax.broadcasted_iota(jnp.int32, (1, tokens), 1)
        all_scores = []
        for i in range(PER):
            r = at * PER + i
            for k in range(pages):
                slot = slots_ref[r, k]
                keys[i, k * page : (k + 1) * page, :] = lat_ref[slot]
                rotated[i, k * page : (k + 1) * page, :] = keyrope_ref[slot]
            packed = packed_ref[r, queries : queries + queries // 2, :]
            half = packed.shape[1] // 2
            q_rope = jnp.concatenate([packed[:, :half], packed[:, half:]], axis=0)
            bias = jnp.where(token < counts[i] * page, 0.0, NEG)
            scores = lax.dot_general(held[r], keys[i, 0:tokens, :], NT, preferred_element_type=jnp.float32)
            scores += lax.dot_general(q_rope, rotated[i, 0:tokens, :], NT, preferred_element_type=jnp.float32)
            all_scores.append(scores + bias)
        for i in range(PER):
            r = at * PER + i
            scores = all_scores[i]
            top = jnp.max(scores, axis=1, keepdims=True)
            weights = jnp.exp2((scores - top) * (scale * math.log2(math.e)))
            total = jnp.sum(weights, axis=1, keepdims=True)
            mixed = jnp.dot(weights.astype(jnp.bfloat16), keys[i, 0:tokens, :], preferred_element_type=jnp.float32)
            held[r] = (mixed * (1.0 / total)).astype(jnp.bfloat16)
            tops[...] = jnp.where(lanes == r, top, tops[...])
            totals[...] = jnp.where(lanes == r, total, totals[...])

    pl.when(most <= 4)(lambda: run(4))
    pl.when((most > 4) & (most <= 6))(lambda: run(6))
    pl.when((most > 6) & (most <= 8))(lambda: run(8))
    pl.when(most > 8)(lambda: run(10))

def share_step(scale, tops, totals, packed):
    rows, _, width = packed.shape
    queries = tops.shape[0]
    lse = tops[...] * scale + jnp.log(jnp.maximum(totals[...], 1e-30))
    lse = lse.T[:rows]
    row = lax.broadcasted_iota(jnp.int32, (rows, 8, width), 1)
    out = jnp.zeros((rows, 8, width), jnp.float32)
    left = lse
    per = queries // width
    for level in range(3):
        piece = left.astype(jnp.bfloat16).astype(jnp.float32)
        left = left - piece
        for c in range(per):
            part = piece[:, c * width : (c + 1) * width].reshape(rows, 1, width)
            out = jnp.where(row == level * per + c, part, out)
    packed[:, queries : queries + 16, :] = jnp.concatenate([out, jnp.zeros_like(out)], axis=1).astype(jnp.bfloat16)

def body(scale, counts_ref, slots_ref, packed_hbm, upk_hbm, lat_hbm, keyrope_hbm, upv_hbm, out_hbm,
         packed, upk, lat, keyrope, upv, held, keys, rotated, tops, totals, in_sems, key_sems, value_sems, out_sems):
    heads = upk.shape[0]
    queries = held.shape[1]
    groups = heads // 4
    chunk = heads // PIECES

    def piece(hbm, vmem, sems, k):
        span = pl.ds(k * chunk, chunk)
        return pltpu.make_async_copy(hbm.at[span], vmem.at[span], sems.at[k])

    def out_copy(at):
        return pltpu.make_async_copy(packed.at[:, sixteen(at), :], out_hbm.at[:, sixteen(at), :], out_sems.at[at])

    load_packed = pltpu.make_async_copy(packed_hbm, packed, in_sems.at[0])
    load_lat = pltpu.make_async_copy(lat_hbm, lat, in_sems.at[1])
    load_rope = pltpu.make_async_copy(keyrope_hbm, keyrope, in_sems.at[2])
    load_packed.start()
    for k in range(PIECES):
        piece(upk_hbm, upk, key_sems, k).start()
    load_lat.start()
    load_rope.start()
    for k in range(PIECES):
        piece(upv_hbm, upv, value_sems, k).start()
    tops[...] = jnp.zeros_like(tops)
    totals[...] = jnp.ones_like(totals)
    load_packed.wait()

    def absorb(at, _):
        @pl.when(at % (groups // PIECES) == 0)
        def _():
            piece(upk_hbm, upk, key_sems, at // (groups // PIECES)).wait()
        absorb_step(at, packed, upk, held)
        return 0
    lax.fori_loop(0, groups, absorb, 0)

    load_lat.wait()
    load_rope.wait()

    def attend(at, _):
        attend_step(scale, at, counts_ref, slots_ref, packed, lat, keyrope, held, keys, rotated, tops, totals)
        return 0
    lax.fori_loop(0, held.shape[0] // PER, attend, 0)

    share_step(scale, tops, totals, packed)
    out_copy(groups).start()
    def project(at, _):
        @pl.when(at % (groups // PIECES) == 0)
        def _():
            piece(upv_hbm, upv, value_sems, at // (groups // PIECES)).wait()
        project_step(at, held, upv, packed)
        out_copy(at).start()
        return 0
    lax.fori_loop(0, groups, project, 0)
    def drain(at, _):
        out_copy(at).wait()
        return 0
    lax.fori_loop(0, groups + 1, drain, 0)

def attention(counts, slots, packed, up_key, up_value, pool_latent, pool_rope, scale):
    rows = packed.shape[0]
    heads, nope, latent = up_key.shape
    value = up_value.shape[2]
    queries = heads * 4
    page = pool_latent.shape[1]
    rope = pool_rope.shape[2]
    anywhere = pl.BlockSpec(memory_space=pl.ANY)
    scalars = pl.BlockSpec(memory_space=pltpu.SMEM)
    return pl.pallas_call(
        functools.partial(body, scale),
        out_shape=jax.ShapeDtypeStruct((rows, queries + 16, value), jnp.bfloat16),
        in_specs=[scalars] * 2 + [anywhere] * 5,
        out_specs=anywhere,
        scratch_shapes=[
            pltpu.VMEM(packed.shape, jnp.bfloat16),
            pltpu.VMEM(up_key.shape, jnp.bfloat16),
            pltpu.VMEM(pool_latent.shape, jnp.bfloat16),
            pltpu.VMEM(pool_rope.shape, jnp.bfloat16),
            pltpu.VMEM(up_value.shape, jnp.bfloat16),
            pltpu.VMEM((rows, queries, latent), jnp.bfloat16),
            pltpu.VMEM((PER, MAX_PAGES * page, latent), jnp.bfloat16),
            pltpu.VMEM((PER, MAX_PAGES * page, rope), jnp.bfloat16),
            pltpu.VMEM((queries, 128), jnp.float32),
            pltpu.VMEM((queries, 128), jnp.float32),
            pltpu.SemaphoreType.DMA((3,)),
            pltpu.SemaphoreType.DMA((PIECES,)),
            pltpu.SemaphoreType.DMA((PIECES,)),
            pltpu.SemaphoreType.DMA((heads // 4 + 1,)),
        ],
        compiler_params=pltpu.CompilerParams(vmem_limit_bytes=VMEM_BYTES),
        name="attention",
    )(counts, slots, packed, up_key, pool_latent, pool_rope, up_value)

def fresh_part(q_nope, q_rope, up_key, up_value, new_latent, new_rope, scale):
    steps, heads, _ = q_nope.shape
    latent = up_key.shape[2]
    absorbed = jnp.einsum(
        "shn,hnl->hsl", q_nope, up_key, preferred_element_type=jnp.float32
    ).astype(jnp.bfloat16)
    scores = (
        jnp.einsum("hsl,tl->hst", absorbed, new_latent, preferred_element_type=jnp.float32)
        + jnp.einsum("she,te->hst", q_rope, new_rope, preferred_element_type=jnp.float32)
    ) * scale
    at = jnp.arange(steps, dtype=jnp.int32)
    allowed = at[None, None, :] <= at[None, :, None]
    scores = jnp.where(allowed, scores, NEG)
    top = jnp.max(scores, axis=2, keepdims=True)
    weights = jnp.where(allowed, jnp.exp(scores - top), 0.0)
    total = jnp.sum(weights, axis=2, keepdims=True)
    mixed = jnp.einsum(
        "hst,tl->hsl", weights.astype(jnp.bfloat16), new_latent, preferred_element_type=jnp.float32
    )
    mixed = (mixed / total).astype(jnp.bfloat16)
    out = jnp.einsum("hsl,hlv->hsv", mixed, up_value, preferred_element_type=jnp.float32)
    return out, (top + jnp.log(total))[:, :, 0]


def page_lists(page_shard, page_slot, shards):
    kept = page_shard.shape[0]
    rank = jnp.sum(
        (page_shard[:, None] == page_shard[None, :])
        & (jnp.arange(kept)[None, :] < jnp.arange(kept)[:, None]),
        axis=1,
    )
    here = page_shard[None, :] == jnp.arange(shards, dtype=jnp.int32)[:, None]
    counts = jnp.sum(here, axis=1).astype(jnp.int32)
    at = jnp.arange(MAX_PAGES)[None, :, None]
    slots = jnp.sum(
        jnp.where(here[:, None, :] & (rank[None, None, :] == at), page_slot[None, None, :], 0),
        axis=2,
    ).astype(jnp.int32)
    return jnp.concatenate(
        [counts[:, None], slots, jnp.zeros((shards, 15 - MAX_PAGES), jnp.int32)], axis=1
    )


def exchange(x):
    return lax.all_to_all(x, "batch", split_axis=0, concat_axis=0, tiled=True)


def per_device(
    q_nope, q_rope, up_key, up_value, pool_latent, pool_rope,
    new_latent, new_rope, page_shard, page_slot
):
    shards = lax.axis_size("batch")
    steps = q_nope.shape[0]
    heads, nope, latent = up_key.shape
    value = up_value.shape[2]
    slots_total, page, _ = pool_latent.shape
    rope = pool_rope.shape[1] // page
    scale = 1.0 / math.sqrt(nope + rope)
    q_nope = q_nope.reshape(steps, heads, nope)
    q_rope = q_rope.reshape(steps, heads, rope)

    nope_rows = q_nope.transpose(1, 0, 2).reshape(heads * steps, nope)
    rope_rows = q_rope.transpose(1, 0, 2).reshape(2, heads * steps // 2, rope)
    rope_rows = rope_rows.transpose(1, 0, 2).reshape(heads * steps // 2, 2 * rope)
    own = jnp.concatenate([nope_rows, rope_rows], axis=0)
    packed = lax.all_gather(own, "batch", axis=0, tiled=False)

    lists = exchange(page_lists(page_shard[0, :, 0], page_slot[0], shards))
    fresh_out, fresh_lse = fresh_part(
        q_nope, q_rope, up_key, up_value, new_latent[:, 0], new_rope.reshape(steps, rope), scale
    )
    pool_rope = pool_rope.reshape(slots_total, page, rope)
    packed, lists, fresh_out, fresh_lse, pool_rope = lax.optimization_barrier(
        (packed, lists, fresh_out, fresh_lse, pool_rope)
    )
    parts = exchange(
        attention(
            lists[:, 0], lists[:, 1 : 1 + MAX_PAGES], packed, up_key, up_value,
            pool_latent, pool_rope, scale,
        )
    )
    queries = heads * steps
    extra = queries // value
    lse = parts[:, queries : queries + 3 * extra].astype(jnp.float32)
    lse = jnp.sum(lse.reshape(shards, 3, queries), axis=1)
    parts = parts[:, :queries]

    fresh_lse = fresh_lse.reshape(1, heads * steps)
    top = jnp.maximum(jnp.max(lse, axis=0, keepdims=True), fresh_lse)
    share = jnp.exp(lse - top)
    fresh_share = jnp.exp(fresh_lse - top)
    total = jnp.sum(share, axis=0, keepdims=True) + fresh_share
    share = share / total
    fresh_share = (fresh_share / total).reshape(heads * steps, 1)
    out = jnp.sum(parts.astype(jnp.float32) * share[:, :, None], axis=0)
    out = out + fresh_share * fresh_out.reshape(heads * steps, value)
    out = out.astype(jnp.bfloat16).reshape(heads, steps, value).transpose(1, 0, 2)
    return out.reshape(steps, 1, heads * value)


def solution(mesh):
    placed = (
        P(None, "batch", "head"),
        P(None, "batch", "head"),
        P("head", None, None),
        P("head", None, None),
        P("batch", None, None),
        P("batch", None),
        P(None, "batch", None),
        P("batch", None),
        P("batch", None, None),
        P("batch", None),
    )
    return jax.shard_map(
        per_device, mesh=mesh, in_specs=placed, out_specs=P(None, "batch", "head"), check_vma=False
    )
```

```python
import functools
import math

import jax
import jax.numpy as jnp
from jax import lax
from jax.experimental import pallas as pl
from jax.experimental.pallas import tpu as pltpu
from jax.sharding import PartitionSpec as P

MAX_PAGES = 10
NEG = -1e30
VMEM_BYTES = 62 * 1024 * 1024
PER = 2
PIECES = 4
NT = (((1,), (1,)), ((), ()))


def sixteen(at):
    return pl.ds(pl.multiple_of(at * 16, 16), 16)

def absorb_step(at, packed, up_ref, held):
    rows, _, nope = packed.shape
    latent = up_ref.shape[2]
    q = packed[:, sixteen(at), :].astype(jnp.float32).reshape(rows, 2, 8, nope)
    first = lax.broadcasted_iota(jnp.int32, (rows, 8, nope), 1) < 4
    halves = []
    for pair in range(2):
        part = q[:, pair]
        wide = jnp.concatenate([jnp.where(first, part, 0.0), jnp.where(first, 0.0, part)], axis=2)
        wide = wide.reshape(rows * 8, 2 * nope).astype(jnp.bfloat16)
        weight = up_ref[pl.ds(at * 4 + 2 * pair, 2)].reshape(2 * nope, latent)
        out = jnp.dot(wide, weight, preferred_element_type=jnp.float32)
        halves.append(out.reshape(rows, 8, latent))
    held[:, sixteen(at), :] = jnp.concatenate(halves, axis=1).astype(jnp.bfloat16)

def project_step(at, held, up_ref, packed):
    rows, _, latent = held.shape
    value = up_ref.shape[2]
    mixed = held[:, sixteen(at), :].astype(jnp.float32).reshape(rows, 2, 8, latent)
    first = lax.broadcasted_iota(jnp.int32, (rows, 8, value), 1) < 4
    halves = []
    for pair in range(2):
        part = mixed[:, pair].reshape(rows * 8, latent).astype(jnp.bfloat16)
        at_head = at * 4 + 2 * pair
        weight = jnp.concatenate([up_ref[at_head], up_ref[at_head + 1]], axis=1)
        out = jnp.dot(part, weight, preferred_element_type=jnp.float32)
        out = out.reshape(rows, 8, 2 * value)
        halves.append(jnp.where(first, out[:, :, :value], out[:, :, value:]))
    packed[:, sixteen(at), :] = jnp.concatenate(halves, axis=1).astype(jnp.bfloat16)

def attend_step(scale, at, counts_ref, slots_ref, order_ref, packed_ref, lat_ref, keyrope_ref, held, keys, rotated, tops, totals):
    queries, latent = held.shape[1:]
    page = lat_ref.shape[1]
    owners = [order_ref[at * PER + i] for i in range(PER)]
    counts = [counts_ref[owners[i]] for i in range(PER)]
    most = functools.reduce(jnp.maximum, counts)

    def run(pages):
        tokens = pages * page
        lanes = lax.broadcasted_iota(jnp.int32, (queries, 128), 1)
        token = lax.broadcasted_iota(jnp.int32, (1, tokens), 1)
        all_scores = []
        for i in range(PER):
            r = at * PER + i
            for k in range(pages):
                slot = slots_ref[owners[i], k]
                keys[i, k * page : (k + 1) * page, :] = lat_ref[slot]
                rotated[i, k * page : (k + 1) * page, :] = keyrope_ref[slot]
            packed = packed_ref[r, queries : queries + queries // 2, :]
            half = packed.shape[1] // 2
            q_rope = jnp.concatenate([packed[:, :half], packed[:, half:]], axis=0)
            bias = jnp.where(token < counts[i] * page, 0.0, NEG)
            scores = lax.dot_general(held[r], keys[i, 0:tokens, :], NT, preferred_element_type=jnp.float32)
            scores += lax.dot_general(q_rope, rotated[i, 0:tokens, :], NT, preferred_element_type=jnp.float32)
            all_scores.append(scores + bias)
        for i in range(PER):
            r = at * PER + i
            scores = all_scores[i]
            top = jnp.max(scores, axis=1, keepdims=True)
            weights = jnp.exp2((scores - top) * (scale * math.log2(math.e)))
            total = jnp.sum(weights, axis=1, keepdims=True)
            mixed = jnp.dot(weights.astype(jnp.bfloat16), keys[i, 0:tokens, :], preferred_element_type=jnp.float32)
            held[r] = (mixed * (1.0 / total)).astype(jnp.bfloat16)
            tops[...] = jnp.where(lanes == r, top, tops[...])
            totals[...] = jnp.where(lanes == r, total, totals[...])

    pl.when(most <= 4)(lambda: run(4))
    pl.when((most > 4) & (most <= 6))(lambda: run(6))
    pl.when((most > 6) & (most <= 8))(lambda: run(8))
    pl.when(most > 8)(lambda: run(10))

def share_step(scale, tops, totals, packed):
    rows, _, width = packed.shape
    queries = tops.shape[0]
    lse = tops[...] * scale + jnp.log(jnp.maximum(totals[...], 1e-30))
    lse = lse.T[:rows]
    row = lax.broadcasted_iota(jnp.int32, (rows, 8, width), 1)
    out = jnp.zeros((rows, 8, width), jnp.float32)
    left = lse
    per = queries // width
    for level in range(3):
        piece = left.astype(jnp.bfloat16).astype(jnp.float32)
        left = left - piece
        for c in range(per):
            part = piece[:, c * width : (c + 1) * width].reshape(rows, 1, width)
            out = jnp.where(row == level * per + c, part, out)
    packed[:, queries : queries + 16, :] = jnp.concatenate([out, jnp.zeros_like(out)], axis=1).astype(jnp.bfloat16)

def body(scale, members, counts_ref, slots_ref, order_ref, *refs):
    packed_hbm, refs = refs[:members], refs[members:]
    upk_hbm, lat_hbm, keyrope_hbm, upv_hbm, refs = refs[:4] + (refs[4:],)
    out_hbm, refs = refs[:members], refs[members:]
    packed, upk, lat, keyrope, upv, held, keys, rotated, tops, totals = refs[:10]
    packed_sems, in_sems, key_sems, value_sems, out_sems = refs[10:]
    heads = upk.shape[0]
    queries = held.shape[1]
    groups = heads // 4
    chunk = heads // PIECES
    each = packed.shape[0] // members
    span = queries // PIECES

    def piece(hbm, vmem, sems, k):
        at = pl.ds(k * chunk, chunk)
        return pltpu.make_async_copy(hbm.at[at], vmem.at[at], sems.at[k])

    def packed_copy(m):
        return pltpu.make_async_copy(packed_hbm[m], packed.at[pl.ds(m * each, each)], packed_sems.at[m])

    def out_copy(k, m):
        if k < PIECES:
            at = pl.ds(k * span, span)
        else:
            at = pl.ds(queries, 16)
        return pltpu.make_async_copy(
            packed.at[pl.ds(m * each, each), at, :], out_hbm[m].at[:, at, :], out_sems.at[k, m]
        )

    load_lat = pltpu.make_async_copy(lat_hbm, lat, in_sems.at[0])
    load_rope = pltpu.make_async_copy(keyrope_hbm, keyrope, in_sems.at[1])
    for m in range(members):
        packed_copy(m).start()
    for k in range(PIECES):
        piece(upk_hbm, upk, key_sems, k).start()
    load_lat.start()
    load_rope.start()
    for k in range(PIECES):
        piece(upv_hbm, upv, value_sems, k).start()
    tops[...] = jnp.zeros_like(tops)
    totals[...] = jnp.ones_like(totals)
    for m in range(members):
        packed_copy(m).wait()

    def absorb(at, _):
        absorb_step(at, packed, upk, held)
        return 0
    for k in range(PIECES):
        piece(upk_hbm, upk, key_sems, k).wait()
        lax.fori_loop(k * groups // PIECES, (k + 1) * groups // PIECES, absorb, 0)

    load_lat.wait()
    load_rope.wait()

    def attend(at, _):
        attend_step(
            scale, at, counts_ref, slots_ref, order_ref, packed, lat, keyrope, held, keys, rotated,
            tops, totals
        )
        return 0
    lax.fori_loop(0, held.shape[0] // PER, attend, 0)

    share_step(scale, tops, totals, packed)
    for m in range(members):
        out_copy(PIECES, m).start()

    def project(at, _):
        project_step(at, held, upv, packed)
        return 0
    for k in range(PIECES):
        piece(upv_hbm, upv, value_sems, k).wait()
        lax.fori_loop(k * groups // PIECES, (k + 1) * groups // PIECES, project, 0)
        for m in range(members):
            out_copy(k, m).start()
    for k in range(PIECES + 1):
        for m in range(members):
            out_copy(k, m).wait()


def attention(lists, order, packed, up_key, up_value, pool_latent, pool_rope, scale):
    members = len(packed)
    each, length, _ = packed[0].shape
    rows = members * each
    heads, _, latent = up_key.shape
    value = up_value.shape[2]
    queries = heads * 4
    page = pool_latent.shape[1]
    rope = pool_rope.shape[2]
    anywhere = pl.BlockSpec(memory_space=pl.ANY)
    scalars = pl.BlockSpec(memory_space=pltpu.SMEM)
    return pl.pallas_call(
        functools.partial(body, scale, members),
        out_shape=[jax.ShapeDtypeStruct((each, queries + 16, value), jnp.bfloat16)] * members,
        in_specs=[scalars] * 3 + [anywhere] * (members + 4),
        out_specs=[anywhere] * members,
        scratch_shapes=[
            pltpu.VMEM((rows, length, value), jnp.bfloat16),
            pltpu.VMEM(up_key.shape, jnp.bfloat16),
            pltpu.VMEM(pool_latent.shape, jnp.bfloat16),
            pltpu.VMEM(pool_rope.shape, jnp.bfloat16),
            pltpu.VMEM(up_value.shape, jnp.bfloat16),
            pltpu.VMEM((rows, queries, latent), jnp.bfloat16),
            pltpu.VMEM((PER, MAX_PAGES * page, latent), jnp.bfloat16),
            pltpu.VMEM((PER, MAX_PAGES * page, rope), jnp.bfloat16),
            pltpu.VMEM((queries, 128), jnp.float32),
            pltpu.VMEM((queries, 128), jnp.float32),
            pltpu.SemaphoreType.DMA((members,)),
            pltpu.SemaphoreType.DMA((2,)),
            pltpu.SemaphoreType.DMA((PIECES,)),
            pltpu.SemaphoreType.DMA((PIECES,)),
            pltpu.SemaphoreType.DMA((PIECES + 1, members)),
        ],
        compiler_params=pltpu.CompilerParams(vmem_limit_bytes=VMEM_BYTES),
        name="attention",
    )(lists[0], lists[1], order, *packed, up_key, pool_latent, pool_rope, up_value)


def fresh_part(q_nope, q_rope, up_key, up_value, new_latent, new_rope, scale):
    steps, heads, _ = q_nope.shape
    latent = up_key.shape[2]
    absorbed = jnp.einsum(
        "shn,hnl->hsl", q_nope, up_key, preferred_element_type=jnp.float32
    ).astype(jnp.bfloat16)
    scores = (
        jnp.einsum("hsl,tl->hst", absorbed, new_latent, preferred_element_type=jnp.float32)
        + jnp.einsum("she,te->hst", q_rope, new_rope, preferred_element_type=jnp.float32)
    ) * scale
    at = jnp.arange(steps, dtype=jnp.int32)
    allowed = at[None, None, :] <= at[None, :, None]
    scores = jnp.where(allowed, scores, NEG)
    top = jnp.max(scores, axis=2, keepdims=True)
    weights = jnp.where(allowed, jnp.exp(scores - top), 0.0)
    total = jnp.sum(weights, axis=2, keepdims=True)
    mixed = jnp.einsum(
        "hst,tl->hsl", weights.astype(jnp.bfloat16), new_latent, preferred_element_type=jnp.float32
    )
    mixed = (mixed / total).astype(jnp.bfloat16)
    out = jnp.einsum("hsl,hlv->hsv", mixed, up_value, preferred_element_type=jnp.float32)
    return out, (top + jnp.log(total))[:, :, 0]


def page_lists(page_shard, page_slot, shards):
    kept = page_shard.shape[0]
    rank = jnp.sum(
        (page_shard[:, None] == page_shard[None, :])
        & (jnp.arange(kept)[None, :] < jnp.arange(kept)[:, None]),
        axis=1,
    )
    here = page_shard[None, :] == jnp.arange(shards, dtype=jnp.int32)[:, None]
    counts = jnp.sum(here, axis=1).astype(jnp.int32)
    at = jnp.arange(MAX_PAGES)[None, :, None]
    slots = jnp.sum(
        jnp.where(here[:, None, :] & (rank[None, None, :] == at), page_slot[None, None, :], 0),
        axis=2,
    ).astype(jnp.int32)
    return jnp.concatenate(
        [counts[:, None], slots, jnp.zeros((shards, 15 - MAX_PAGES), jnp.int32)], axis=1
    )


def exchange(x):
    return lax.all_to_all(x, "batch", split_axis=0, concat_axis=0, tiled=True)


SIDE = 4
CORNERS = [(a, b, c) for a in range(2) for b in range(2) for c in range(2)]


def place(index):
    return (index // (SIDE * SIDE), index // SIDE % SIDE, index % SIDE)


def index_of(at):
    return (at[0] * SIDE + at[1]) * SIDE + at[2]


def flipped(v, core):
    return (v + 1 - 2 * ((v - core) % 2)) % SIDE


def across(at, core, corner):
    return tuple(flipped(v, core) if f else v for v, f in zip(at, corner))


def strided(at, corner):
    return tuple((v + 2 * f) % SIDE for v, f in zip(at, corner))


def block_pairs(corner, cores):
    pairs = []
    for i in range(SIDE**3):
        for core in range(cores):
            j = index_of(across(place(i), core, corner))
            pairs.append((i * cores + core, j * cores + core))
    return pairs


def stride_pairs(corner):
    return [(i, index_of(strided(place(i), corner))) for i in range(SIDE**3)]


def to_block(x, corner):
    return lax.ppermute(x, ("batch", "head"), block_pairs(corner, lax.axis_size("head")))


def to_stride(x, corner):
    return lax.ppermute(x, "batch", stride_pairs(corner))


def row_order():
    at, core = place(lax.axis_index("batch")), lax.axis_index("head")
    order = [index_of(strided(across(at, core, m), e)) for m in CORNERS for e in CORNERS]
    return jnp.stack(order).astype(jnp.int32)


def unpack(part, queries):
    extra = queries // part.shape[2]
    lse = part[:, queries : queries + 3 * extra].astype(jnp.float32)
    lse = jnp.sum(lse.reshape(part.shape[0], 3, queries), axis=1)
    return part[:, :queries].astype(jnp.float32), lse


def mix(outs, lses):
    top = functools.reduce(jnp.maximum, lses)
    shares = [jnp.exp(lse - top) for lse in lses]
    total = sum(shares)
    out = sum(out * (share / total)[:, :, None] for out, share in zip(outs, shares))
    return out, top + jnp.log(total)


def pack(out, lse):
    rows, queries, value = out.shape
    pieces, left = [], lse
    for _ in range(3):
        piece = lax.reduce_precision(left, 8, 7)
        left = left - piece
        pieces.append(piece.reshape(rows, queries // value, value))
    extra = 16 - 3 * queries // value
    pieces.append(jnp.zeros((rows, extra, value), jnp.float32))
    return jnp.concatenate([out] + pieces, axis=1).astype(jnp.bfloat16)


def per_device(
    q_nope, q_rope, up_key, up_value, pool_latent, pool_rope,
    new_latent, new_rope, page_shard, page_slot
):
    shards = lax.axis_size("batch")
    steps = q_nope.shape[0]
    heads, nope, latent = up_key.shape
    value = up_value.shape[2]
    slots_total, page, _ = pool_latent.shape
    rope = pool_rope.shape[1] // page
    scale = 1.0 / math.sqrt(nope + rope)
    q_nope = q_nope.reshape(steps, heads, nope)
    q_rope = q_rope.reshape(steps, heads, rope)

    nope_rows = q_nope.transpose(1, 0, 2).reshape(heads * steps, nope)
    rope_rows = q_rope.transpose(1, 0, 2).reshape(2, heads * steps // 2, rope)
    rope_rows = rope_rows.transpose(1, 0, 2).reshape(heads * steps // 2, 2 * rope)
    own = jnp.concatenate([nope_rows, rope_rows], axis=0)
    near = jnp.stack([own] + [to_stride(own, e) for e in CORNERS[1:]])
    packed = [near] + [to_block(near, m) for m in CORNERS[1:]]

    lists = exchange(page_lists(page_shard[0, :, 0], page_slot[0], shards))
    fresh_out, fresh_lse = fresh_part(
        q_nope, q_rope, up_key, up_value, new_latent[:, 0], new_rope.reshape(steps, rope), scale
    )
    pool_rope = pool_rope.reshape(slots_total, page, rope)
    counts, slots = lists[:, 0], lists[:, 1 : 1 + MAX_PAGES]
    packed, counts, slots, fresh_out, fresh_lse, pool_rope = lax.optimization_barrier(
        (packed, counts, slots, fresh_out, fresh_lse, pool_rope)
    )
    parts = attention(
        (counts, slots), row_order(), packed, up_key, up_value, pool_latent, pool_rope, scale
    )

    queries = heads * steps
    parts = [parts[0]] + [to_block(part, m) for part, m in zip(parts[1:], CORNERS[1:])]
    outs, lses = zip(*(unpack(part, queries) for part in parts))
    mixed = pack(*mix(outs, lses))
    rows = [mixed[:1]] + [to_stride(mixed[k : k + 1], CORNERS[k]) for k in range(1, len(CORNERS))]
    outs, lses = zip(*(unpack(row, queries) for row in rows))
    outs += (fresh_out.reshape(1, queries, value),)
    lses += (fresh_lse.reshape(1, queries),)
    out, _ = mix(outs, lses)
    out = out.astype(jnp.bfloat16).reshape(heads, steps, value).transpose(1, 0, 2)
    return out.reshape(steps, 1, heads * value)


def solution(mesh):
    placed = (
        P(None, "batch", "head"),
        P(None, "batch", "head"),
        P("head", None, None),
        P("head", None, None),
        P("batch", None, None),
        P("batch", None),
        P(None, "batch", None),
        P("batch", None),
        P("batch", None, None),
        P("batch", None),
    )
    return jax.shard_map(
        per_device, mesh=mesh, in_specs=placed, out_specs=P(None, "batch", "head"), check_vma=False
    )
```

```python
import functools
import math

import jax
import jax.numpy as jnp
from jax import lax
from jax.experimental import pallas as pl
from jax.experimental.pallas import tpu as pltpu
from jax.sharding import PartitionSpec as P

MAX_PAGES = 10
NEG = -1e30
VMEM_BYTES = 52 * 1024 * 1024
PER = 2
PIECES = 4
NT = (((1,), (1,)), ((), ()))


def sixteen(at):
    return pl.ds(pl.multiple_of(at * 16, 16), 16)

def absorb_step(at, packed, up_ref, held):
    rows, _, nope = packed.shape
    latent = up_ref.shape[2]
    q = packed[:, sixteen(at), :].astype(jnp.float32).reshape(rows, 2, 8, nope)
    first = lax.broadcasted_iota(jnp.int32, (rows, 8, nope), 1) < 4
    halves = []
    for pair in range(2):
        part = q[:, pair]
        wide = jnp.concatenate([jnp.where(first, part, 0.0), jnp.where(first, 0.0, part)], axis=2)
        wide = wide.reshape(rows * 8, 2 * nope).astype(jnp.bfloat16)
        weight = up_ref[pl.ds(at * 4 + 2 * pair, 2)].reshape(2 * nope, latent)
        out = jnp.dot(wide, weight, preferred_element_type=jnp.float32)
        halves.append(out.reshape(rows, 8, latent))
    held[:, sixteen(at), :] = jnp.concatenate(halves, axis=1).astype(jnp.bfloat16)

def project_step(at, held, up_ref, packed):
    rows, _, latent = held.shape
    value = up_ref.shape[2]
    mixed = held[:, sixteen(at), :].astype(jnp.float32).reshape(rows, 2, 8, latent)
    first = lax.broadcasted_iota(jnp.int32, (rows, 8, value), 1) < 4
    halves = []
    for pair in range(2):
        part = mixed[:, pair].reshape(rows * 8, latent).astype(jnp.bfloat16)
        at_head = at * 4 + 2 * pair
        weight = jnp.concatenate([up_ref[at_head], up_ref[at_head + 1]], axis=1)
        out = jnp.dot(part, weight, preferred_element_type=jnp.float32)
        out = out.reshape(rows, 8, 2 * value)
        halves.append(jnp.where(first, out[:, :, :value], out[:, :, value:]))
    packed[:, sixteen(at), :] = jnp.concatenate(halves, axis=1).astype(jnp.bfloat16)

def attend_step(scale, at, lists_ref, packed_ref, lat_ref, keyrope_ref, held, keys, rotated, tops, totals):
    queries, latent = held.shape[1:]
    page = lat_ref.shape[1]
    counts = [lists_ref[at * PER + i, 0] for i in range(PER)]
    most = functools.reduce(jnp.maximum, counts)

    def run(pages):
        tokens = pages * page
        lanes = lax.broadcasted_iota(jnp.int32, (queries, 128), 1)
        token = lax.broadcasted_iota(jnp.int32, (1, tokens), 1)
        all_scores = []
        for i in range(PER):
            r = at * PER + i
            for k in range(pages):
                slot = lists_ref[r, 1 + k]
                keys[i, k * page : (k + 1) * page, :] = lat_ref[slot]
                rotated[i, k * page : (k + 1) * page, :] = keyrope_ref[slot]
            packed = packed_ref[r, queries : queries + queries // 2, :]
            half = packed.shape[1] // 2
            q_rope = jnp.concatenate([packed[:, :half], packed[:, half:]], axis=0)
            bias = jnp.where(token < counts[i] * page, 0.0, NEG)
            scores = lax.dot_general(held[r], keys[i, 0:tokens, :], NT, preferred_element_type=jnp.float32)
            scores += lax.dot_general(q_rope, rotated[i, 0:tokens, :], NT, preferred_element_type=jnp.float32)
            all_scores.append(scores + bias)
        for i in range(PER):
            r = at * PER + i
            scores = all_scores[i]
            top = jnp.max(scores, axis=1, keepdims=True)
            weights = jnp.exp2((scores - top) * (scale * math.log2(math.e)))
            total = jnp.sum(weights, axis=1, keepdims=True)
            mixed = jnp.dot(weights.astype(jnp.bfloat16), keys[i, 0:tokens, :], preferred_element_type=jnp.float32)
            held[r] = (mixed * (1.0 / total)).astype(jnp.bfloat16)
            tops[...] = jnp.where(lanes == r, top, tops[...])
            totals[...] = jnp.where(lanes == r, total, totals[...])

    pl.when(most <= 4)(lambda: run(4))
    pl.when((most > 4) & (most <= 6))(lambda: run(6))
    pl.when((most > 6) & (most <= 8))(lambda: run(8))
    pl.when(most > 8)(lambda: run(10))

def share_step(scale, tops, totals, packed):
    rows, _, width = packed.shape
    queries = tops.shape[0]
    lse = tops[...] * scale + jnp.log(jnp.maximum(totals[...], 1e-30))
    lse = lse.T[:rows]
    row = lax.broadcasted_iota(jnp.int32, (rows, 8, width), 1)
    out = jnp.zeros((rows, 8, width), jnp.float32)
    left = lse
    per = queries // width
    for level in range(3):
        piece = left.astype(jnp.bfloat16).astype(jnp.float32)
        left = left - piece
        for c in range(per):
            part = piece[:, c * width : (c + 1) * width].reshape(rows, 1, width)
            out = jnp.where(row == level * per + c, part, out)
    packed[:, queries : queries + 16, :] = jnp.concatenate([out, jnp.zeros_like(out)], axis=1).astype(jnp.bfloat16)

def body(scale, lists_ref, packed_hbm, upk_hbm, lat_hbm, keyrope_hbm, upv_hbm, out_hbm,
         packed, upk, lat, keyrope, upv, held, keys, rotated, tops, totals, in_sems, key_sems, value_sems, out_sems):
    heads = upk.shape[0]
    queries = held.shape[1]
    groups = heads // 4
    chunk = heads // PIECES

    def piece(hbm, vmem, sems, k):
        span = pl.ds(k * chunk, chunk)
        return pltpu.make_async_copy(hbm.at[span], vmem.at[span], sems.at[k])

    def out_copy(at):
        return pltpu.make_async_copy(packed.at[:, sixteen(at), :], out_hbm.at[:, sixteen(at), :], out_sems.at[at])

    load_packed = pltpu.make_async_copy(
        packed_hbm.at[:, pl.ds(0, packed.shape[1]), :], packed, in_sems.at[0]
    )
    load_lat = pltpu.make_async_copy(lat_hbm, lat, in_sems.at[1])
    load_rope = pltpu.make_async_copy(keyrope_hbm, keyrope, in_sems.at[2])
    load_packed.start()
    for k in range(PIECES):
        piece(upk_hbm, upk, key_sems, k).start()
    load_lat.start()
    load_rope.start()
    for k in range(PIECES):
        piece(upv_hbm, upv, value_sems, k).start()
    tops[...] = jnp.zeros_like(tops)
    totals[...] = jnp.ones_like(totals)
    load_packed.wait()

    def absorb(at, _):
        @pl.when(at % (groups // PIECES) == 0)
        def _():
            piece(upk_hbm, upk, key_sems, at // (groups // PIECES)).wait()
        absorb_step(at, packed, upk, held)
        return 0
    lax.fori_loop(0, groups, absorb, 0)

    load_lat.wait()
    load_rope.wait()

    def attend(at, _):
        attend_step(scale, at, lists_ref, packed, lat, keyrope, held, keys, rotated, tops, totals)
        return 0
    lax.fori_loop(0, held.shape[0] // PER, attend, 0)

    share_step(scale, tops, totals, packed)
    out_copy(groups).start()
    def project(at, _):
        @pl.when(at % (groups // PIECES) == 0)
        def _():
            piece(upv_hbm, upv, value_sems, at // (groups // PIECES)).wait()
        project_step(at, held, upv, packed)
        out_copy(at).start()
        return 0
    lax.fori_loop(0, groups, project, 0)
    def drain(at, _):
        out_copy(at).wait()
        return 0
    lax.fori_loop(0, groups + 1, drain, 0)

def attention(lists, packed, up_key, up_value, pool_latent, pool_rope, scale):
    rows = packed.shape[0]
    heads, nope, latent = up_key.shape
    value = up_value.shape[2]
    queries = heads * 4
    page = pool_latent.shape[1]
    rope = pool_rope.shape[2]
    anywhere = pl.BlockSpec(memory_space=pl.ANY)
    scalars = pl.BlockSpec(memory_space=pltpu.SMEM)
    return pl.pallas_call(
        functools.partial(body, scale),
        out_shape=jax.ShapeDtypeStruct((rows, queries + 16, value), jnp.bfloat16),
        in_specs=[scalars] + [anywhere] * 5,
        out_specs=anywhere,
        scratch_shapes=[
            pltpu.VMEM((rows, queries + queries // 2, nope), jnp.bfloat16),
            pltpu.VMEM(up_key.shape, jnp.bfloat16),
            pltpu.VMEM(pool_latent.shape, jnp.bfloat16),
            pltpu.VMEM(pool_rope.shape, jnp.bfloat16),
            pltpu.VMEM(up_value.shape, jnp.bfloat16),
            pltpu.VMEM((rows, queries, latent), jnp.bfloat16),
            pltpu.VMEM((PER, MAX_PAGES * page, latent), jnp.bfloat16),
            pltpu.VMEM((PER, MAX_PAGES * page, rope), jnp.bfloat16),
            pltpu.VMEM((queries, 128), jnp.float32),
            pltpu.VMEM((queries, 128), jnp.float32),
            pltpu.SemaphoreType.DMA((3,)),
            pltpu.SemaphoreType.DMA((PIECES,)),
            pltpu.SemaphoreType.DMA((PIECES,)),
            pltpu.SemaphoreType.DMA((heads // 4 + 1,)),
        ],
        compiler_params=pltpu.CompilerParams(vmem_limit_bytes=VMEM_BYTES),
        cost_estimate=pl.CostEstimate(
            flops=rows * queries * 640 * 4 * latent, bytes_accessed=1 << 27, transcendentals=0
        ),
        name="attention",
    )(lists, packed, up_key, pool_latent, pool_rope, up_value)

def fresh_part(q_nope, q_rope, up_key, up_value, new_latent, new_rope, scale):
    steps, heads, _ = q_nope.shape
    latent = up_key.shape[2]
    absorbed = jnp.einsum(
        "shn,hnl->hsl", q_nope, up_key, preferred_element_type=jnp.float32
    ).astype(jnp.bfloat16)
    scores = (
        jnp.einsum("hsl,tl->hst", absorbed, new_latent, preferred_element_type=jnp.float32)
        + jnp.einsum("she,te->hst", q_rope, new_rope, preferred_element_type=jnp.float32)
    ) * scale
    at = jnp.arange(steps, dtype=jnp.int32)
    allowed = at[None, None, :] <= at[None, :, None]
    scores = jnp.where(allowed, scores, NEG)
    top = jnp.max(scores, axis=2, keepdims=True)
    weights = jnp.where(allowed, jnp.exp(scores - top), 0.0)
    total = jnp.sum(weights, axis=2, keepdims=True)
    mixed = jnp.einsum(
        "hst,tl->hsl", weights.astype(jnp.bfloat16), new_latent, preferred_element_type=jnp.float32
    )
    mixed = (mixed / total).astype(jnp.bfloat16)
    out = jnp.einsum("hsl,hlv->hsv", mixed, up_value, preferred_element_type=jnp.float32)
    return out, (top + jnp.log(total))[:, :, 0]


def page_lists(page_shard, page_slot, shards):
    kept = page_shard.shape[0]
    rank = jnp.sum(
        (page_shard[:, None] == page_shard[None, :])
        & (jnp.arange(kept)[None, :] < jnp.arange(kept)[:, None]),
        axis=1,
    )
    here = page_shard[None, :] == jnp.arange(shards, dtype=jnp.int32)[:, None]
    counts = jnp.sum(here, axis=1).astype(jnp.int32)
    at = jnp.arange(MAX_PAGES)[None, :, None]
    slots = jnp.sum(
        jnp.where(here[:, None, :] & (rank[None, None, :] == at), page_slot[None, None, :], 0),
        axis=2,
    ).astype(jnp.int32)
    return jnp.concatenate(
        [counts[:, None], slots, jnp.zeros((shards, 15 - MAX_PAGES), jnp.int32)], axis=1
    )


SIDE = 4
HALVES = 2


def corner_index(bits):
    return (bits[0] * 2 + bits[1]) * 2 + bits[2]


def grouped(cores, key):
    groups = {}
    for i in range(SIDE**3):
        at = (i // (SIDE * SIDE), i // SIDE % SIDE, i % SIDE)
        for core in range(cores):
            group, position = key(at, core)
            groups.setdefault((core,) + group, {})[corner_index(position)] = i * cores + core
    return [[group[p] for p in sorted(group)] for _, group in sorted(groups.items())]


def sublattice(at, core):
    return tuple(v % 2 for v in at), tuple(v // 2 for v in at)


def block(at, core):
    return tuple((v - core) % SIDE // 2 for v in at), tuple((v - core) % 2 for v in at)


def exchange(x, key):
    groups = grouped(lax.axis_size("head"), key)
    return lax.all_to_all(
        x, ("batch", "head"), split_axis=0, concat_axis=0, tiled=True, axis_index_groups=groups
    )


def spread(x, key):
    return exchange(jnp.broadcast_to(x[None], (8,) + x.shape), key)


def mix(parts, queries, fresh=None):
    count, rows, _, value = parts.shape
    extra = queries // value
    lse = parts[:, :, queries : queries + 3 * extra].astype(jnp.float32)
    lse = jnp.sum(lse.reshape(count, rows, 3, queries), axis=2)
    top = jnp.max(lse, axis=0)
    if fresh is not None:
        top = jnp.maximum(top, fresh[1])
    share = jnp.exp(lse - top)
    total = jnp.sum(share, axis=0)
    if fresh is not None:
        fresh_share = jnp.exp(fresh[1] - top)
        total = total + fresh_share
    out = jnp.sum(
        parts[:, :, :queries].astype(jnp.float32) * (share / total)[..., None], axis=0
    )
    if fresh is not None:
        out = out + fresh[0] * (fresh_share / total)[..., None]
    return out, top + jnp.log(total)


def pack(out, lse):
    rows, queries, value = out.shape
    pieces, left = [], lse
    for _ in range(3):
        piece = lax.reduce_precision(left, 8, 7)
        left = left - piece
        pieces.append(piece.reshape(rows, queries // value, value))
    extra = 16 - 3 * queries // value
    pieces.append(jnp.zeros((rows, extra, value), jnp.float32))
    return jnp.concatenate([out] + pieces, axis=1).astype(jnp.bfloat16)


def per_device(
    q_nope, q_rope, up_key, up_value, pool_latent, pool_rope,
    new_latent, new_rope, page_shard, page_slot
):
    shards = lax.axis_size("batch")
    steps = q_nope.shape[0]
    heads, nope, latent = up_key.shape
    value = up_value.shape[2]
    slots_total, page, _ = pool_latent.shape
    rope = pool_rope.shape[1] // page
    scale = 1.0 / math.sqrt(nope + rope)
    q_nope = q_nope.reshape(steps, heads, nope)
    q_rope = q_rope.reshape(steps, heads, rope)

    nope_rows = q_nope.transpose(1, 0, 2).reshape(heads * steps, nope)
    rope_rows = q_rope.transpose(1, 0, 2).reshape(2, heads * steps // 2, rope)
    rope_rows = rope_rows.transpose(1, 0, 2).reshape(heads * steps // 2, 2 * rope)
    lists = page_lists(page_shard[0, :, 0], page_slot[0], shards)
    wide = lists.shape[1]
    list_rows = lists.astype(jnp.bfloat16).reshape(shards * wide // nope, nope)
    list_rows = jnp.pad(list_rows, ((0, 16 - list_rows.shape[0]), (0, 0)))
    own = jnp.concatenate([nope_rows, rope_rows, list_rows], axis=0)
    queries = heads * steps
    length = queries + queries // 2

    near = spread(own, sublattice)
    count = near.shape[0] // HALVES
    pool_rope = pool_rope.reshape(slots_total, page, rope)
    me = lax.axis_index("batch")
    gathered = [
        spread(near[k * count : (k + 1) * count], block) for k in range(HALVES)
    ]
    fresh = fresh_part(
        q_nope, q_rope, up_key, up_value, new_latent[:, 0], new_rope.reshape(steps, rope), scale
    )
    returned = []
    for k in range(HALVES):
        packed = gathered[k].reshape(8 * count, own.shape[0], nope)
        lists = packed[:, length : length + shards * wide // nope]
        lists = lists.reshape(8 * count, shards, wide)
        lists = lax.dynamic_index_in_dim(lists, me, 1, keepdims=False).astype(jnp.int32)
        parts = attention(lists, packed, up_key, up_value, pool_latent, pool_rope, scale)
        if k + 1 < HALVES:
            parts, gathered[k + 1] = lax.optimization_barrier((parts, gathered[k + 1]))
        parts = exchange(parts.reshape(8, count, queries + 16, value), block)
        returned.append(pack(*mix(parts, queries)))
    rows = exchange(jnp.concatenate(returned, axis=0), sublattice)
    fresh = (fresh[0].reshape(1, queries, value), fresh[1].reshape(1, queries))
    out, _ = mix(rows[:, None], queries, fresh)
    out = out.astype(jnp.bfloat16).reshape(heads, steps, value).transpose(1, 0, 2)
    return out.reshape(steps, 1, heads * value)


def solution(mesh):
    placed = (
        P(None, "batch", "head"),
        P(None, "batch", "head"),
        P("head", None, None),
        P("head", None, None),
        P("batch", None, None),
        P("batch", None),
        P(None, "batch", None),
        P("batch", None),
        P("batch", None, None),
        P("batch", None),
    )
    return jax.shard_map(
        per_device, mesh=mesh, in_specs=placed, out_specs=P(None, "batch", "head"), check_vma=False
    )
```

```python
import functools
import math

import jax
import jax.numpy as jnp
from jax import lax
from jax.experimental import pallas as pl
from jax.experimental.pallas import tpu as pltpu
from jax.sharding import PartitionSpec as P

MAX_PAGES = 10
NEG = -1e30
VMEM_BYTES = 52 * 1024 * 1024
PER = 2
PIECES = 4
NT = (((1,), (1,)), ((), ()))


def sixteen(at):
    return pl.ds(pl.multiple_of(at * 16, 16), 16)

def absorb_step(at, packed, up_ref, held):
    rows, _, nope = packed.shape
    latent = up_ref.shape[2]
    q = packed[:, sixteen(at), :].astype(jnp.float32).reshape(rows, 2, 8, nope)
    first = lax.broadcasted_iota(jnp.int32, (rows, 8, nope), 1) < 4
    halves = []
    for pair in range(2):
        part = q[:, pair]
        wide = jnp.concatenate([jnp.where(first, part, 0.0), jnp.where(first, 0.0, part)], axis=2)
        wide = wide.reshape(rows * 8, 2 * nope).astype(jnp.bfloat16)
        weight = up_ref[pl.ds(at * 4 + 2 * pair, 2)].reshape(2 * nope, latent)
        out = jnp.dot(wide, weight, preferred_element_type=jnp.float32)
        halves.append(out.reshape(rows, 8, latent))
    held[:, sixteen(at), :] = jnp.concatenate(halves, axis=1).astype(jnp.bfloat16)

def project_step(at, held, up_ref, packed):
    rows, _, latent = held.shape
    value = up_ref.shape[2]
    mixed = held[:, sixteen(at), :].astype(jnp.float32).reshape(rows, 2, 8, latent)
    first = lax.broadcasted_iota(jnp.int32, (rows, 8, value), 1) < 4
    halves = []
    for pair in range(2):
        part = mixed[:, pair].reshape(rows * 8, latent).astype(jnp.bfloat16)
        at_head = at * 4 + 2 * pair
        weight = jnp.concatenate([up_ref[at_head], up_ref[at_head + 1]], axis=1)
        out = jnp.dot(part, weight, preferred_element_type=jnp.float32)
        out = out.reshape(rows, 8, 2 * value)
        halves.append(jnp.where(first, out[:, :, :value], out[:, :, value:]))
    packed[:, sixteen(at), :] = jnp.concatenate(halves, axis=1).astype(jnp.bfloat16)

def attend_step(scale, at, lists_ref, packed_ref, lat_ref, keyrope_ref, held, keys, rotated, tops, totals):
    queries, latent = held.shape[1:]
    page = lat_ref.shape[1]
    counts = [lists_ref[at * PER + i, 0] for i in range(PER)]
    most = functools.reduce(jnp.maximum, counts)

    def run(pages):
        tokens = pages * page
        lanes = lax.broadcasted_iota(jnp.int32, (queries, 128), 1)
        token = lax.broadcasted_iota(jnp.int32, (1, tokens), 1)
        all_scores = []
        for i in range(PER):
            r = at * PER + i
            for k in range(pages):
                slot = lists_ref[r, 1 + k]
                keys[i, k * page : (k + 1) * page, :] = lat_ref[slot]
                rotated[i, k * page : (k + 1) * page, :] = keyrope_ref[slot]
            packed = packed_ref[r, queries : queries + queries // 2, :]
            half = packed.shape[1] // 2
            q_rope = jnp.concatenate([packed[:, :half], packed[:, half:]], axis=0)
            bias = jnp.where(token < counts[i] * page, 0.0, NEG)
            scores = lax.dot_general(held[r], keys[i, 0:tokens, :], NT, preferred_element_type=jnp.float32)
            scores += lax.dot_general(q_rope, rotated[i, 0:tokens, :half], NT, preferred_element_type=jnp.float32)
            all_scores.append(scores + bias)
        for i in range(PER):
            r = at * PER + i
            scores = all_scores[i]
            top = jnp.max(scores, axis=1, keepdims=True)
            weights = jnp.exp2((scores - top) * (scale * math.log2(math.e)))
            total = jnp.sum(weights, axis=1, keepdims=True)
            mixed = jnp.dot(weights.astype(jnp.bfloat16), keys[i, 0:tokens, :], preferred_element_type=jnp.float32)
            held[r] = (mixed * (1.0 / total)).astype(jnp.bfloat16)
            tops[...] = jnp.where(lanes == r, top, tops[...])
            totals[...] = jnp.where(lanes == r, total, totals[...])

    pl.when(most <= 4)(lambda: run(4))
    pl.when((most > 4) & (most <= 6))(lambda: run(6))
    pl.when((most > 6) & (most <= 8))(lambda: run(8))
    pl.when(most > 8)(lambda: run(10))

def share_step(scale, tops, totals, packed):
    rows, _, width = packed.shape
    queries = tops.shape[0]
    lse = tops[...] * scale + jnp.log(jnp.maximum(totals[...], 1e-30))
    lse = lse.T[:rows]
    row = lax.broadcasted_iota(jnp.int32, (rows, 8, width), 1)
    out = jnp.zeros((rows, 8, width), jnp.float32)
    left = lse
    per = queries // width
    for level in range(3):
        piece = left.astype(jnp.bfloat16).astype(jnp.float32)
        left = left - piece
        for c in range(per):
            part = piece[:, c * width : (c + 1) * width].reshape(rows, 1, width)
            out = jnp.where(row == level * per + c, part, out)
    packed[:, queries : queries + 16, :] = jnp.concatenate([out, jnp.zeros_like(out)], axis=1).astype(jnp.bfloat16)

def body(scale, lists_ref, packed_hbm, upk_hbm, lat_hbm, keyrope_hbm, upv_hbm, out_hbm,
         packed, upk, lat, keyrope, upv, held, keys, rotated, tops, totals, in_sems, key_sems, value_sems, out_sems):
    heads = upk.shape[0]
    queries = held.shape[1]
    groups = heads // 4
    chunk = heads // PIECES

    def piece(hbm, vmem, sems, k):
        span = pl.ds(k * chunk, chunk)
        return pltpu.make_async_copy(hbm.at[span], vmem.at[span], sems.at[k])

    def out_copy(at):
        return pltpu.make_async_copy(packed.at[:, sixteen(at), :], out_hbm.at[:, sixteen(at), :], out_sems.at[at])

    load_packed = pltpu.make_async_copy(
        packed_hbm.at[:, pl.ds(0, packed.shape[1]), :], packed, in_sems.at[0]
    )
    load_lat = pltpu.make_async_copy(lat_hbm, lat, in_sems.at[1])
    load_rope = pltpu.make_async_copy(keyrope_hbm, keyrope, in_sems.at[2])
    load_packed.start()
    for k in range(PIECES):
        piece(upk_hbm, upk, key_sems, k).start()
    load_lat.start()
    load_rope.start()
    for k in range(PIECES):
        piece(upv_hbm, upv, value_sems, k).start()
    tops[...] = jnp.zeros_like(tops)
    totals[...] = jnp.ones_like(totals)
    load_packed.wait()

    def absorb(at, _):
        @pl.when(at % (groups // PIECES) == 0)
        def _():
            piece(upk_hbm, upk, key_sems, at // (groups // PIECES)).wait()
        absorb_step(at, packed, upk, held)
        return 0
    lax.fori_loop(0, groups, absorb, 0)

    load_lat.wait()
    load_rope.wait()

    def attend(at, _):
        attend_step(scale, at, lists_ref, packed, lat, keyrope, held, keys, rotated, tops, totals)
        return 0
    lax.fori_loop(0, held.shape[0] // PER, attend, 0)

    share_step(scale, tops, totals, packed)
    out_copy(groups).start()
    def project(at, _):
        @pl.when(at % (groups // PIECES) == 0)
        def _():
            piece(upv_hbm, upv, value_sems, at // (groups // PIECES)).wait()
        project_step(at, held, upv, packed)
        out_copy(at).start()
        return 0
    lax.fori_loop(0, groups, project, 0)
    def drain(at, _):
        out_copy(at).wait()
        return 0
    lax.fori_loop(0, groups + 1, drain, 0)

def attention(lists, packed, up_key, up_value, pool_latent, pool_rope, scale):
    rows = packed.shape[0]
    heads, nope, latent = up_key.shape
    value = up_value.shape[2]
    queries = heads * 4
    page = pool_latent.shape[1]
    rope = pool_rope.shape[2]
    anywhere = pl.BlockSpec(memory_space=pl.ANY)
    scalars = pl.BlockSpec(memory_space=pltpu.SMEM)
    return pl.pallas_call(
        functools.partial(body, scale),
        out_shape=jax.ShapeDtypeStruct((rows, queries + 16, value), jnp.bfloat16),
        in_specs=[scalars] + [anywhere] * 5,
        out_specs=anywhere,
        scratch_shapes=[
            pltpu.VMEM((rows, queries + queries // 2, nope), jnp.bfloat16),
            pltpu.VMEM(up_key.shape, jnp.bfloat16),
            pltpu.VMEM(pool_latent.shape, jnp.bfloat16),
            pltpu.VMEM(pool_rope.shape, jnp.bfloat16),
            pltpu.VMEM(up_value.shape, jnp.bfloat16),
            pltpu.VMEM((rows, queries, latent), jnp.bfloat16),
            pltpu.VMEM((PER, MAX_PAGES * page, latent), jnp.bfloat16),
            pltpu.VMEM((PER, MAX_PAGES * page, rope), jnp.bfloat16),
            pltpu.VMEM((queries, 128), jnp.float32),
            pltpu.VMEM((queries, 128), jnp.float32),
            pltpu.SemaphoreType.DMA((3,)),
            pltpu.SemaphoreType.DMA((PIECES,)),
            pltpu.SemaphoreType.DMA((PIECES,)),
            pltpu.SemaphoreType.DMA((heads // 4 + 1,)),
        ],
        compiler_params=pltpu.CompilerParams(vmem_limit_bytes=VMEM_BYTES),
        cost_estimate=pl.CostEstimate(
            flops=rows * queries * 640 * 4 * latent, bytes_accessed=1 << 27, transcendentals=0
        ),
        name="attention",
    )(lists, packed, up_key, pool_latent, pool_rope, up_value)

def fresh_part(q_nope, q_rope, up_key, up_value, new_latent, new_rope, scale):
    steps, heads, _ = q_nope.shape
    latent = up_key.shape[2]
    absorbed = jnp.einsum(
        "shn,hnl->hsl", q_nope, up_key, preferred_element_type=jnp.float32
    ).astype(jnp.bfloat16)
    scores = (
        jnp.einsum("hsl,tl->hst", absorbed, new_latent, preferred_element_type=jnp.float32)
        + jnp.einsum("she,te->hst", q_rope, new_rope, preferred_element_type=jnp.float32)
    ) * scale
    at = jnp.arange(steps, dtype=jnp.int32)
    allowed = at[None, None, :] <= at[None, :, None]
    scores = jnp.where(allowed, scores, NEG)
    top = jnp.max(scores, axis=2, keepdims=True)
    weights = jnp.where(allowed, jnp.exp(scores - top), 0.0)
    total = jnp.sum(weights, axis=2, keepdims=True)
    mixed = jnp.einsum(
        "hst,tl->hsl", weights.astype(jnp.bfloat16), new_latent, preferred_element_type=jnp.float32
    )
    mixed = (mixed / total).astype(jnp.bfloat16)
    out = jnp.einsum("hsl,hlv->hsv", mixed, up_value, preferred_element_type=jnp.float32)
    return out, (top + jnp.log(total))[:, :, 0]


def page_lists(page_shard, page_slot, shards):
    kept = page_shard.shape[0]
    rank = jnp.sum(
        (page_shard[:, None] == page_shard[None, :])
        & (jnp.arange(kept)[None, :] < jnp.arange(kept)[:, None]),
        axis=1,
    )
    here = page_shard[None, :] == jnp.arange(shards, dtype=jnp.int32)[:, None]
    counts = jnp.sum(here, axis=1).astype(jnp.int32)
    at = jnp.arange(MAX_PAGES)[None, :, None]
    slots = jnp.sum(
        jnp.where(here[:, None, :] & (rank[None, None, :] == at), page_slot[None, None, :], 0),
        axis=2,
    ).astype(jnp.int32)
    return jnp.concatenate(
        [counts[:, None], slots, jnp.zeros((shards, 15 - MAX_PAGES), jnp.int32)], axis=1
    )


SIDE = 4
HALVES = 2


def corner_index(bits):
    return (bits[0] * 2 + bits[1]) * 2 + bits[2]


def grouped(cores, key):
    groups = {}
    for i in range(SIDE**3):
        at = (i // (SIDE * SIDE), i // SIDE % SIDE, i % SIDE)
        for core in range(cores):
            group, position = key(at, core)
            groups.setdefault((core,) + group, {})[corner_index(position)] = i * cores + core
    return [[group[p] for p in sorted(group)] for _, group in sorted(groups.items())]


def sublattice(at, core):
    return tuple(v % 2 for v in at), tuple(v // 2 for v in at)


def block(at, core):
    return tuple((v - core) % SIDE // 2 for v in at), tuple((v - core) % 2 for v in at)


def exchange(x, key):
    groups = grouped(lax.axis_size("head"), key)
    return lax.all_to_all(
        x, ("batch", "head"), split_axis=0, concat_axis=0, tiled=True, axis_index_groups=groups
    )


def spread(x, key):
    return exchange(jnp.broadcast_to(x[None], (8,) + x.shape), key)


def mix(parts, queries, fresh=None):
    count, rows, _, value = parts.shape
    extra = queries // value
    lse = parts[:, :, queries : queries + 3 * extra].astype(jnp.float32)
    lse = jnp.sum(lse.reshape(count, rows, 3, queries), axis=2)
    top = jnp.max(lse, axis=0)
    if fresh is not None:
        top = jnp.maximum(top, fresh[1])
    share = jnp.exp(lse - top)
    total = jnp.sum(share, axis=0)
    if fresh is not None:
        fresh_share = jnp.exp(fresh[1] - top)
        total = total + fresh_share
    out = jnp.sum(
        parts[:, :, :queries].astype(jnp.float32) * (share / total)[..., None], axis=0
    )
    if fresh is not None:
        out = out + fresh[0] * (fresh_share / total)[..., None]
    return out, top + jnp.log(total)


def pack(out, lse):
    rows, queries, value = out.shape
    pieces, left = [], lse
    for _ in range(3):
        piece = lax.reduce_precision(left, 8, 7)
        left = left - piece
        pieces.append(piece.reshape(rows, queries // value, value))
    extra = 16 - 3 * queries // value
    pieces.append(jnp.zeros((rows, extra, value), jnp.float32))
    return jnp.concatenate([out] + pieces, axis=1).astype(jnp.bfloat16)


def per_device(
    q_nope, q_rope, up_key, up_value, pool_latent, pool_rope,
    new_latent, new_rope, page_shard, page_slot
):
    shards = lax.axis_size("batch")
    steps = q_nope.shape[0]
    heads, nope, latent = up_key.shape
    value = up_value.shape[2]
    slots_total, page, _ = pool_latent.shape
    rope = pool_rope.shape[1] // page
    scale = 1.0 / math.sqrt(nope + rope)
    q_nope = q_nope.reshape(steps, heads, nope)
    q_rope = q_rope.reshape(steps, heads, rope)

    nope_rows = q_nope.transpose(1, 0, 2).reshape(heads * steps, nope)
    rope_rows = q_rope.transpose(1, 0, 2).reshape(2, heads * steps // 2, rope)
    rope_rows = rope_rows.transpose(1, 0, 2).reshape(heads * steps // 2, 2 * rope)
    lists = page_lists(page_shard[0, :, 0], page_slot[0], shards)
    wide = lists.shape[1]
    list_rows = lists.astype(jnp.bfloat16).reshape(shards * wide // nope, nope)
    list_rows = jnp.pad(list_rows, ((0, 16 - list_rows.shape[0]), (0, 0)))
    own = jnp.concatenate([nope_rows, rope_rows, list_rows], axis=0)
    queries = heads * steps
    length = queries + queries // 2

    near = spread(own, sublattice)
    count = 8 // HALVES
    pool_rope = pool_rope.reshape(slots_total, page, rope)
    pool_rope = jnp.pad(pool_rope, ((0, 0), (0, 0), (0, 128 - rope)))
    near, pool_rope = lax.optimization_barrier((near, pool_rope))
    me = lax.axis_index("batch")
    gathered = [
        spread(near[k * count : (k + 1) * count], block) for k in range(HALVES)
    ]
    fresh = fresh_part(
        q_nope, q_rope, up_key, up_value, new_latent[:, 0], new_rope.reshape(steps, rope), scale
    )
    returned = []
    for k in range(HALVES):
        packed = gathered[k].reshape(8 * count, own.shape[0], nope)
        lists = packed[:, length : length + shards * wide // nope]
        lists = lists.reshape(8 * count, shards, wide)
        lists = lax.dynamic_index_in_dim(lists, me, 1, keepdims=False).astype(jnp.int32)
        parts = attention(lists, packed, up_key, up_value, pool_latent, pool_rope, scale)
        if k + 1 < HALVES:
            parts, gathered[k + 1] = lax.optimization_barrier((parts, gathered[k + 1]))
        parts = exchange(parts.reshape(8, count, queries + 16, value), block)
        returned.append(parts)
    mixed = pack(*mix(returned[0], queries))
    mixed, second = lax.optimization_barrier((mixed, returned[1]))
    rows = jnp.concatenate([mixed, pack(*mix(second, queries))], axis=0)
    rows = exchange(rows, sublattice)
    fresh = (fresh[0].reshape(1, queries, value), fresh[1].reshape(1, queries))
    out, _ = mix(rows[:, None], queries, fresh)
    out = lax.optimization_barrier(out.astype(jnp.bfloat16))
    out = out.reshape(heads, steps, value).transpose(1, 0, 2)
    return out.reshape(steps, 1, heads * value)


def solution(mesh):
    placed = (
        P(None, "batch", "head"),
        P(None, "batch", "head"),
        P("head", None, None),
        P("head", None, None),
        P("batch", None, None),
        P("batch", None),
        P(None, "batch", None),
        P("batch", None),
        P("batch", None, None),
        P("batch", None),
    )
    return jax.shard_map(
        per_device, mesh=mesh, in_specs=placed, out_specs=P(None, "batch", "head"), check_vma=False
    )
```

```python
import functools
import math

import jax
import jax.numpy as jnp
from jax import lax
from jax.experimental import pallas as pl
from jax.experimental.pallas import tpu as pltpu
from jax.sharding import PartitionSpec as P

MAX_PAGES = 10
NEG = -1e30
VMEM_BYTES = 54 * 1024 * 1024
PER = 4
PIECES = 4
NT = (((1,), (1,)), ((), ()))


def sixteen(at):
    return pl.ds(pl.multiple_of(at * 16, 16), 16)

def absorb_step(at, packed, up_ref, held):
    rows, _, nope = packed.shape
    latent = up_ref.shape[2]
    q = packed[:, sixteen(at), :].astype(jnp.float32).reshape(rows, 2, 8, nope)
    first = lax.broadcasted_iota(jnp.int32, (rows, 8, nope), 1) < 4
    halves = []
    for pair in range(2):
        part = q[:, pair]
        wide = jnp.concatenate([jnp.where(first, part, 0.0), jnp.where(first, 0.0, part)], axis=2)
        wide = wide.reshape(rows * 8, 2 * nope).astype(jnp.bfloat16)
        weight = up_ref[pl.ds(at * 4 + 2 * pair, 2)].reshape(2 * nope, latent)
        out = jnp.dot(wide, weight, preferred_element_type=jnp.float32)
        halves.append(out.reshape(rows, 8, latent))
    held[:, sixteen(at), :] = jnp.concatenate(halves, axis=1).astype(jnp.bfloat16)

def project_step(at, held, up_ref, packed):
    rows, _, latent = held.shape
    value = up_ref.shape[2]
    mixed = held[:, sixteen(at), :].astype(jnp.float32).reshape(rows, 2, 8, latent)
    first = lax.broadcasted_iota(jnp.int32, (rows, 8, value), 1) < 4
    halves = []
    for pair in range(2):
        part = mixed[:, pair].reshape(rows * 8, latent).astype(jnp.bfloat16)
        at_head = at * 4 + 2 * pair
        weight = jnp.concatenate([up_ref[at_head], up_ref[at_head + 1]], axis=1)
        out = jnp.dot(part, weight, preferred_element_type=jnp.float32)
        out = out.reshape(rows, 8, 2 * value)
        halves.append(jnp.where(first, out[:, :, :value], out[:, :, value:]))
    packed[:, sixteen(at), :] = jnp.concatenate(halves, axis=1).astype(jnp.bfloat16)

def attend_step(scale, at, lists_ref, packed_ref, lat_ref, keyrope_ref, held, keys, rotated, tops, totals):
    queries, latent = held.shape[1:]
    page = lat_ref.shape[1]
    counts = [lists_ref[at * PER + i, 0] for i in range(PER)]
    most = functools.reduce(jnp.maximum, counts)

    def run(pages):
        tokens = pages * page
        lanes = lax.broadcasted_iota(jnp.int32, (queries, 128), 1)
        token = lax.broadcasted_iota(jnp.int32, (1, tokens), 1)
        all_scores = []
        for i in range(PER):
            r = at * PER + i
            for k in range(pages):
                slot = lists_ref[r, 1 + k]
                keys[i, k * page : (k + 1) * page, :] = lat_ref[slot]
                rotated[i, k * page : (k + 1) * page, :] = keyrope_ref[slot]
            packed = packed_ref[r, queries : queries + queries // 2, :]
            half = packed.shape[1] // 2
            q_rope = jnp.concatenate([packed[:, :half], packed[:, half:]], axis=0)
            bias = jnp.where(token < counts[i] * page, 0.0, NEG)
            scores = lax.dot_general(held[r], keys[i, 0:tokens, :], NT, preferred_element_type=jnp.float32)
            scores += lax.dot_general(q_rope, rotated[i, 0:tokens, :half], NT, preferred_element_type=jnp.float32)
            all_scores.append(scores + bias)
        for i in range(PER):
            r = at * PER + i
            scores = all_scores[i]
            top = jnp.max(scores, axis=1, keepdims=True)
            weights = jnp.exp2((scores - top) * (scale * math.log2(math.e)))
            total = jnp.sum(weights, axis=1, keepdims=True)
            mixed = jnp.dot(weights.astype(jnp.bfloat16), keys[i, 0:tokens, :], preferred_element_type=jnp.float32)
            held[r] = (mixed * (1.0 / total)).astype(jnp.bfloat16)
            tops[...] = jnp.where(lanes == r, top, tops[...])
            totals[...] = jnp.where(lanes == r, total, totals[...])

    pl.when(most <= 4)(lambda: run(4))
    pl.when((most > 4) & (most <= 6))(lambda: run(6))
    pl.when((most > 6) & (most <= 8))(lambda: run(8))
    pl.when(most > 8)(lambda: run(10))

def share_step(scale, tops, totals, packed):
    rows, _, width = packed.shape
    queries = tops.shape[0]
    lse = tops[...] * scale + jnp.log(jnp.maximum(totals[...], 1e-30))
    lse = lse.T[:rows]
    row = lax.broadcasted_iota(jnp.int32, (rows, 8, width), 1)
    out = jnp.zeros((rows, 8, width), jnp.float32)
    left = lse
    per = queries // width
    for level in range(3):
        piece = left.astype(jnp.bfloat16).astype(jnp.float32)
        left = left - piece
        for c in range(per):
            part = piece[:, c * width : (c + 1) * width].reshape(rows, 1, width)
            out = jnp.where(row == level * per + c, part, out)
    packed[:, queries : queries + 16, :] = jnp.concatenate([out, jnp.zeros_like(out)], axis=1).astype(jnp.bfloat16)

def body(scale, lists_ref, packed_hbm, upk_hbm, lat_hbm, keyrope_hbm, upv_hbm, out_hbm,
         packed, upk, lat, keyrope, upv, held, keys, rotated, tops, totals, in_sems, key_sems, value_sems, out_sems):
    heads = upk.shape[0]
    queries = held.shape[1]
    groups = heads // 4
    chunk = heads // PIECES

    def piece(hbm, vmem, sems, k):
        span = pl.ds(k * chunk, chunk)
        return pltpu.make_async_copy(hbm.at[span], vmem.at[span], sems.at[k])

    def out_copy(at):
        return pltpu.make_async_copy(packed.at[:, sixteen(at), :], out_hbm.at[:, sixteen(at), :], out_sems.at[at])

    load_packed = pltpu.make_async_copy(
        packed_hbm.at[:, pl.ds(0, packed.shape[1]), :], packed, in_sems.at[0]
    )
    load_lat = pltpu.make_async_copy(lat_hbm, lat, in_sems.at[1])
    load_rope = pltpu.make_async_copy(keyrope_hbm, keyrope, in_sems.at[2])
    load_packed.start()
    for k in range(PIECES):
        piece(upk_hbm, upk, key_sems, k).start()
    load_lat.start()
    load_rope.start()
    tops[...] = jnp.zeros_like(tops)
    totals[...] = jnp.ones_like(totals)
    load_packed.wait()

    def absorb(k, _):
        piece(upk_hbm, upk, key_sems, k).wait()
        for j in range(groups // PIECES):
            absorb_step(k * (groups // PIECES) + j, packed, upk, held)
        return 0

    lax.fori_loop(0, PIECES, absorb, 0)

    load_lat.wait()
    load_rope.wait()
    for k in range(PIECES):
        piece(upv_hbm, upv, value_sems, k).start()

    def attend(at, _):
        attend_step(scale, at, lists_ref, packed, lat, keyrope, held, keys, rotated, tops, totals)
        return 0
    lax.fori_loop(0, held.shape[0] // PER, attend, 0)

    share_step(scale, tops, totals, packed)
    out_copy(groups).start()
    def project(k, _):
        piece(upv_hbm, upv, value_sems, k).wait()
        for j in range(groups // PIECES):
            at = k * (groups // PIECES) + j
            project_step(at, held, upv, packed)
            out_copy(at).start()
        return 0

    lax.fori_loop(0, PIECES, project, 0)

    def drain(at, _):
        out_copy(at).wait()
        return 0
    lax.fori_loop(0, groups + 1, drain, 0)

def attention(lists, packed, up_key, up_value, pool_latent, pool_rope, scale):
    rows = packed.shape[0]
    heads, nope, latent = up_key.shape
    value = up_value.shape[2]
    queries = heads * 4
    page = pool_latent.shape[1]
    rope = pool_rope.shape[2]
    anywhere = pl.BlockSpec(memory_space=pl.ANY)
    scalars = pl.BlockSpec(memory_space=pltpu.SMEM)
    return pl.pallas_call(
        functools.partial(body, scale),
        out_shape=jax.ShapeDtypeStruct((rows, queries + 16, value), jnp.bfloat16),
        in_specs=[scalars] + [anywhere] * 5,
        out_specs=anywhere,
        scratch_shapes=[
            pltpu.VMEM((rows, queries + queries // 2, nope), jnp.bfloat16),
            pltpu.VMEM(up_key.shape, jnp.bfloat16),
            pltpu.VMEM(pool_latent.shape, jnp.bfloat16),
            pltpu.VMEM(pool_rope.shape, jnp.bfloat16),
            pltpu.VMEM(up_value.shape, jnp.bfloat16),
            pltpu.VMEM((rows, queries, latent), jnp.bfloat16),
            pltpu.VMEM((PER, MAX_PAGES * page, latent), jnp.bfloat16),
            pltpu.VMEM((PER, MAX_PAGES * page, rope), jnp.bfloat16),
            pltpu.VMEM((queries, 128), jnp.float32),
            pltpu.VMEM((queries, 128), jnp.float32),
            pltpu.SemaphoreType.DMA((3,)),
            pltpu.SemaphoreType.DMA((PIECES,)),
            pltpu.SemaphoreType.DMA((PIECES,)),
            pltpu.SemaphoreType.DMA((heads // 4 + 1,)),
        ],
        compiler_params=pltpu.CompilerParams(vmem_limit_bytes=VMEM_BYTES),
        cost_estimate=pl.CostEstimate(
            flops=rows * queries * 640 * 4 * latent, bytes_accessed=1 << 27, transcendentals=0
        ),
        name="attention",
    )(lists, packed, up_key, pool_latent, pool_rope, up_value)


def fresh_part(q_nope, q_rope, up_key, up_value, new_latent, new_rope, scale):
    steps, heads, _ = q_nope.shape
    latent = up_key.shape[2]
    absorbed = jnp.einsum(
        "shn,hnl->hsl", q_nope, up_key, preferred_element_type=jnp.float32
    ).astype(jnp.bfloat16)
    scores = (
        jnp.einsum("hsl,tl->hst", absorbed, new_latent, preferred_element_type=jnp.float32)
        + jnp.einsum("she,te->hst", q_rope, new_rope, preferred_element_type=jnp.float32)
    ) * scale
    at = jnp.arange(steps, dtype=jnp.int32)
    allowed = at[None, None, :] <= at[None, :, None]
    scores = jnp.where(allowed, scores, NEG)
    top = jnp.max(scores, axis=2, keepdims=True)
    weights = jnp.where(allowed, jnp.exp(scores - top), 0.0)
    total = jnp.sum(weights, axis=2, keepdims=True)
    mixed = jnp.einsum(
        "hst,tl->hsl", weights.astype(jnp.bfloat16), new_latent, preferred_element_type=jnp.float32
    )
    mixed = (mixed / total).astype(jnp.bfloat16)
    out = jnp.einsum("hsl,hlv->hsv", mixed, up_value, preferred_element_type=jnp.float32)
    return out, (top + jnp.log(total))[:, :, 0]


def page_lists(page_shard, page_slot, shards):
    kept = page_shard.shape[0]
    rank = jnp.sum(
        (page_shard[:, None] == page_shard[None, :])
        & (jnp.arange(kept)[None, :] < jnp.arange(kept)[:, None]),
        axis=1,
    )
    here = page_shard[None, :] == jnp.arange(shards, dtype=jnp.int32)[:, None]
    counts = jnp.sum(here, axis=1).astype(jnp.int32)
    at = jnp.arange(MAX_PAGES)[None, :, None]
    slots = jnp.sum(
        jnp.where(here[:, None, :] & (rank[None, None, :] == at), page_slot[None, None, :], 0),
        axis=2,
    ).astype(jnp.int32)
    return jnp.concatenate(
        [counts[:, None], slots, jnp.zeros((shards, 15 - MAX_PAGES), jnp.int32)], axis=1
    )


SIDE = 4
HALVES = 2


def corner_index(bits):
    return (bits[0] * 2 + bits[1]) * 2 + bits[2]


def grouped(cores, key):
    groups = {}
    for i in range(SIDE**3):
        at = (i // (SIDE * SIDE), i // SIDE % SIDE, i % SIDE)
        for core in range(cores):
            group, position = key(at, core)
            groups.setdefault((core,) + group, {})[corner_index(position)] = i * cores + core
    return [[group[p] for p in sorted(group)] for _, group in sorted(groups.items())]


def sublattice(at, core):
    return tuple(v % 2 for v in at), tuple(v // 2 for v in at)


def block(at, core):
    return tuple((v - core) % SIDE // 2 for v in at), tuple((v - core) % 2 for v in at)


def exchange(x, key):
    groups = grouped(lax.axis_size("head"), key)
    return lax.all_to_all(
        x, ("batch", "head"), split_axis=0, concat_axis=0, tiled=True, axis_index_groups=groups
    )


def spread(x, key):
    return exchange(jnp.broadcast_to(x[None], (8,) + x.shape), key)


def mix(parts, queries, fresh=None):
    count, rows, _, value = parts.shape
    extra = queries // value
    lse = parts[:, :, queries : queries + 3 * extra].astype(jnp.float32)
    lse = jnp.sum(lse.reshape(count, rows, 3, queries), axis=2)
    top = jnp.max(lse, axis=0)
    if fresh is not None:
        top = jnp.maximum(top, fresh[1])
    share = jnp.exp(lse - top)
    total = jnp.sum(share, axis=0)
    if fresh is not None:
        fresh_share = jnp.exp(fresh[1] - top)
        total = total + fresh_share
    out = jnp.sum(
        parts[:, :, :queries].astype(jnp.float32) * (share / total)[..., None], axis=0
    )
    if fresh is not None:
        out = out + fresh[0] * (fresh_share / total)[..., None]
    return out, top + jnp.log(total)


def pack(out, lse):
    rows, queries, value = out.shape
    pieces, left = [], lse
    for _ in range(3):
        piece = lax.reduce_precision(left, 8, 7)
        left = left - piece
        pieces.append(piece.reshape(rows, queries // value, value))
    extra = 16 - 3 * queries // value
    pieces.append(jnp.zeros((rows, extra, value), jnp.float32))
    return jnp.concatenate([out] + pieces, axis=1).astype(jnp.bfloat16)


def per_device(
    q_nope, q_rope, up_key, up_value, pool_latent, pool_rope,
    new_latent, new_rope, page_shard, page_slot
):
    shards = lax.axis_size("batch")
    steps = q_nope.shape[0]
    heads, nope, latent = up_key.shape
    value = up_value.shape[2]
    slots_total, page, _ = pool_latent.shape
    rope = pool_rope.shape[1] // page
    scale = 1.0 / math.sqrt(nope + rope)
    q_nope = q_nope.reshape(steps, heads, nope)
    q_rope = q_rope.reshape(steps, heads, rope)

    nope_rows = q_nope.transpose(1, 0, 2).reshape(heads * steps, nope)
    rope_rows = q_rope.transpose(1, 0, 2).reshape(2, heads * steps // 2, rope)
    rope_rows = rope_rows.transpose(1, 0, 2).reshape(heads * steps // 2, 2 * rope)
    lists = page_lists(page_shard[0, :, 0], page_slot[0], shards)
    wide = lists.shape[1]
    list_rows = lists.astype(jnp.bfloat16).reshape(shards * wide // nope, nope)
    list_rows = jnp.pad(list_rows, ((0, 16 - list_rows.shape[0]), (0, 0)))
    own = jnp.concatenate([nope_rows, rope_rows, list_rows], axis=0)
    queries = heads * steps
    length = queries + queries // 2

    near = spread(own, sublattice)
    count = 8 // HALVES
    pool_rope = pool_rope.reshape(slots_total, page, rope)
    pool_rope = jnp.pad(pool_rope, ((0, 0), (0, 0), (0, 128 - rope)))
    fresh = fresh_part(
        q_nope, q_rope, up_key, up_value, new_latent[:, 0], new_rope.reshape(steps, rope), scale
    )
    near, pool_rope, fresh = lax.optimization_barrier((near, pool_rope, fresh))
    me = lax.axis_index("batch")
    gathered = [
        spread(near[k * count : (k + 1) * count], block) for k in range(HALVES)
    ]
    returned = []
    for k in range(HALVES):
        packed = gathered[k].reshape(8 * count, own.shape[0], nope)
        lists = packed[:, length : length + shards * wide // nope]
        lists = lists.reshape(8 * count, shards, wide)
        lists = lax.dynamic_index_in_dim(lists, me, 1, keepdims=False).astype(jnp.int32)
        parts = attention(lists, packed, up_key, up_value, pool_latent, pool_rope, scale)
        if k + 1 < HALVES:
            parts, gathered[k + 1] = lax.optimization_barrier((parts, gathered[k + 1]))
        parts = exchange(parts.reshape(8, count, queries + 16, value), block)
        returned.append(parts)
    mixed = pack(*mix(returned[0], queries))
    mixed, second = lax.optimization_barrier((mixed, returned[1]))
    rows = jnp.concatenate([mixed, pack(*mix(second, queries))], axis=0)
    rows = exchange(rows, sublattice)
    fresh = (fresh[0].reshape(1, queries, value), fresh[1].reshape(1, queries))
    out, _ = mix(rows[:, None], queries, fresh)
    out = lax.optimization_barrier(out.astype(jnp.bfloat16))
    out = out.reshape(heads, steps, value).transpose(1, 0, 2)
    return out.reshape(steps, 1, heads * value)


def solution(mesh):
    placed = (
        P(None, "batch", "head"),
        P(None, "batch", "head"),
        P("head", None, None),
        P("head", None, None),
        P("batch", None, None),
        P("batch", None),
        P(None, "batch", None),
        P("batch", None),
        P("batch", None, None),
        P("batch", None),
    )
    return jax.shard_map(
        per_device, mesh=mesh, in_specs=placed, out_specs=P(None, "batch", "head"), check_vma=False
    )
```

```python
import functools
import math

import jax
import jax.numpy as jnp
from jax import lax
from jax.experimental import pallas as pl
from jax.experimental.pallas import tpu as pltpu
from jax.sharding import PartitionSpec as P

MAX_PAGES = 10
NEG = -1e30
VMEM_BYTES = 60 * 1024 * 1024
PER = 4
PIECES = 4
NT = (((1,), (1,)), ((), ()))


def sixteen(at):
    return pl.ds(pl.multiple_of(at * 16, 16), 16)

def absorb_step(at, packed, up_ref, held):
    rows, _, nope = packed.shape
    latent = up_ref.shape[2]
    q = packed[:, sixteen(at), :].astype(jnp.float32).reshape(rows, 2, 8, nope)
    first = lax.broadcasted_iota(jnp.int32, (rows, 8, nope), 1) < 4
    halves = []
    for pair in range(2):
        part = q[:, pair]
        wide = jnp.concatenate([jnp.where(first, part, 0.0), jnp.where(first, 0.0, part)], axis=2)
        wide = wide.reshape(rows * 8, 2 * nope).astype(jnp.bfloat16)
        weight = up_ref[pl.ds(at * 4 + 2 * pair, 2)].reshape(2 * nope, latent)
        out = jnp.dot(wide, weight, preferred_element_type=jnp.float32)
        halves.append(out.reshape(rows, 8, latent))
    held[:, sixteen(at), :] = jnp.concatenate(halves, axis=1).astype(jnp.bfloat16)

def project_step(at, held, up_ref, packed):
    rows, _, latent = held.shape
    value = up_ref.shape[2]
    mixed = held[:, sixteen(at), :].astype(jnp.float32).reshape(rows, 2, 8, latent)
    first = lax.broadcasted_iota(jnp.int32, (rows, 8, value), 1) < 4
    halves = []
    for pair in range(2):
        part = mixed[:, pair].reshape(rows * 8, latent).astype(jnp.bfloat16)
        at_head = at * 4 + 2 * pair
        weight = jnp.concatenate([up_ref[at_head], up_ref[at_head + 1]], axis=1)
        out = jnp.dot(part, weight, preferred_element_type=jnp.float32)
        out = out.reshape(rows, 8, 2 * value)
        halves.append(jnp.where(first, out[:, :, :value], out[:, :, value:]))
    packed[:, sixteen(at), :] = jnp.concatenate(halves, axis=1).astype(jnp.bfloat16)

def attend_step(scale, at, lists_ref, shift, packed_ref, lat_ref, keyrope_ref, held, keys, rotated, tops, totals):
    queries, latent = held.shape[1:]
    page = lat_ref.shape[1]
    counts = [lists_ref[at * PER + i, shift] for i in range(PER)]
    most = functools.reduce(jnp.maximum, counts)

    def run(pages):
        tokens = pages * page
        lanes = lax.broadcasted_iota(jnp.int32, (queries, 128), 1)
        token = lax.broadcasted_iota(jnp.int32, (1, tokens), 1)
        all_scores = []
        for i in range(PER):
            r = at * PER + i
            for k in range(pages):
                slot = lists_ref[r, shift + 1 + k]
                keys[i, k * page : (k + 1) * page, :] = lat_ref[slot]
                rotated[i, k * page : (k + 1) * page, :] = keyrope_ref[slot]
            packed = packed_ref[r, queries : queries + queries // 2, :]
            half = packed.shape[1] // 2
            q_rope = jnp.concatenate([packed[:, :half], packed[:, half:]], axis=0)
            bias = jnp.where(token < counts[i] * page, 0.0, NEG)
            scores = lax.dot_general(held[r], keys[i, 0:tokens, :], NT, preferred_element_type=jnp.float32)
            scores += lax.dot_general(q_rope, rotated[i, 0:tokens, :half], NT, preferred_element_type=jnp.float32)
            all_scores.append(scores + bias)
        for i in range(PER):
            r = at * PER + i
            scores = all_scores[i]
            top = jnp.max(scores, axis=1, keepdims=True)
            weights = jnp.exp2((scores - top) * (scale * math.log2(math.e)))
            total = jnp.sum(weights, axis=1, keepdims=True)
            mixed = jnp.dot(weights.astype(jnp.bfloat16), keys[i, 0:tokens, :], preferred_element_type=jnp.float32)
            held[r] = (mixed * (1.0 / total)).astype(jnp.bfloat16)
            tops[...] = jnp.where(lanes == r, top, tops[...])
            totals[...] = jnp.where(lanes == r, total, totals[...])

    pl.when(most <= 4)(lambda: run(4))
    pl.when((most > 4) & (most <= 6))(lambda: run(6))
    pl.when((most > 6) & (most <= 8))(lambda: run(8))
    pl.when(most > 8)(lambda: run(10))

def share_step(scale, tops, totals, packed):
    rows, _, width = packed.shape
    queries = tops.shape[0]
    lse = tops[...] * scale + jnp.log(jnp.maximum(totals[...], 1e-30))
    lse = lse.T[:rows]
    row = lax.broadcasted_iota(jnp.int32, (rows, 8, width), 1)
    out = jnp.zeros((rows, 8, width), jnp.float32)
    left = lse
    per = queries // width
    for level in range(3):
        piece = left.astype(jnp.bfloat16).astype(jnp.float32)
        left = left - piece
        for c in range(per):
            part = piece[:, c * width : (c + 1) * width].reshape(rows, 1, width)
            out = jnp.where(row == level * per + c, part, out)
    packed[:, queries : queries + 16, :] = jnp.concatenate([out, jnp.zeros_like(out)], axis=1).astype(jnp.bfloat16)

def body(scale, lists_ref, place_ref, packed_hbm, upk_hbm, lat_hbm, keyrope_hbm, upv_hbm, out_hbm,
         packed, upk, lat, keyrope, upv, held, keys, rotated, tops, totals, in_sems, key_sems, value_sems, out_sems):
    heads = upk.shape[0]
    queries = held.shape[1]
    groups = heads // 4
    chunk = heads // PIECES

    def piece(hbm, vmem, sems, k):
        span = pl.ds(k * chunk, chunk)
        return pltpu.make_async_copy(hbm.at[span], vmem.at[span], sems.at[k])

    def out_copy(at):
        return pltpu.make_async_copy(packed.at[:, sixteen(at), :], out_hbm.at[:, sixteen(at), :], out_sems.at[at])

    load_packed = pltpu.make_async_copy(
        packed_hbm.at[:, pl.ds(0, packed.shape[1]), :], packed, in_sems.at[0]
    )
    load_lat = pltpu.make_async_copy(lat_hbm, lat, in_sems.at[1])
    load_rope = pltpu.make_async_copy(keyrope_hbm, keyrope, in_sems.at[2])
    load_packed.start()
    for k in range(PIECES):
        piece(upk_hbm, upk, key_sems, k).start()
    load_lat.start()
    load_rope.start()
    tops[...] = jnp.zeros_like(tops)
    totals[...] = jnp.ones_like(totals)
    load_packed.wait()

    def absorb(k, _):
        piece(upk_hbm, upk, key_sems, k).wait()
        for j in range(groups // PIECES):
            absorb_step(k * (groups // PIECES) + j, packed, upk, held)
        return 0

    lax.fori_loop(0, PIECES, absorb, 0)

    load_lat.wait()
    load_rope.wait()
    for k in range(PIECES):
        piece(upv_hbm, upv, value_sems, k).start()

    def attend(at, _):
        @pl.when(at != place_ref[0])
        def _():
            attend_step(
                scale, at, lists_ref, place_ref[1], packed, lat, keyrope, held, keys, rotated, tops, totals
            )
        return 0

    lax.fori_loop(0, held.shape[0] // PER, attend, 0)

    share_step(scale, tops, totals, packed)
    out_copy(groups).start()
    def project(k, _):
        piece(upv_hbm, upv, value_sems, k).wait()
        for j in range(groups // PIECES):
            at = k * (groups // PIECES) + j
            project_step(at, held, upv, packed)
            out_copy(at).start()
        return 0

    lax.fori_loop(0, PIECES, project, 0)

    def drain(at, _):
        out_copy(at).wait()
        return 0
    lax.fori_loop(0, groups + 1, drain, 0)

def attention(lists, place, packed, up_key, up_value, pool_latent, pool_rope, scale):
    rows = packed.shape[0]
    heads, nope, latent = up_key.shape
    value = up_value.shape[2]
    queries = heads * 4
    page = pool_latent.shape[1]
    rope = pool_rope.shape[2]
    anywhere = pl.BlockSpec(memory_space=pl.ANY)
    scalars = pl.BlockSpec(memory_space=pltpu.SMEM)
    return pl.pallas_call(
        functools.partial(body, scale),
        out_shape=jax.ShapeDtypeStruct((rows, queries + 16, value), jnp.bfloat16),
        in_specs=[scalars] * 2 + [anywhere] * 5,
        out_specs=anywhere,
        scratch_shapes=[
            pltpu.VMEM((rows, queries + queries // 2, nope), jnp.bfloat16),
            pltpu.VMEM(up_key.shape, jnp.bfloat16),
            pltpu.VMEM(pool_latent.shape, jnp.bfloat16),
            pltpu.VMEM(pool_rope.shape, jnp.bfloat16),
            pltpu.VMEM(up_value.shape, jnp.bfloat16),
            pltpu.VMEM((rows, queries, latent), jnp.bfloat16),
            pltpu.VMEM((PER, MAX_PAGES * page, latent), jnp.bfloat16),
            pltpu.VMEM((PER, MAX_PAGES * page, rope), jnp.bfloat16),
            pltpu.VMEM((queries, 128), jnp.float32),
            pltpu.VMEM((queries, 128), jnp.float32),
            pltpu.SemaphoreType.DMA((3,)),
            pltpu.SemaphoreType.DMA((PIECES,)),
            pltpu.SemaphoreType.DMA((PIECES,)),
            pltpu.SemaphoreType.DMA((heads // 4 + 1,)),
        ],
        compiler_params=pltpu.CompilerParams(vmem_limit_bytes=VMEM_BYTES),
        cost_estimate=pl.CostEstimate(
            flops=rows * queries * 640 * 4 * latent, bytes_accessed=1 << 27, transcendentals=0
        ),
        name="attention",
    )(lists, place, packed, up_key, pool_latent, pool_rope, up_value)


def fresh_part(q_nope, q_rope, up_key, up_value, new_latent, new_rope, scale):
    steps, heads, _ = q_nope.shape
    latent = up_key.shape[2]
    absorbed = jnp.einsum(
        "shn,hnl->hsl", q_nope, up_key, preferred_element_type=jnp.float32
    ).astype(jnp.bfloat16)
    scores = (
        jnp.einsum("hsl,tl->hst", absorbed, new_latent, preferred_element_type=jnp.float32)
        + jnp.einsum("she,te->hst", q_rope, new_rope, preferred_element_type=jnp.float32)
    ) * scale
    at = jnp.arange(steps, dtype=jnp.int32)
    allowed = at[None, None, :] <= at[None, :, None]
    scores = jnp.where(allowed, scores, NEG)
    top = jnp.max(scores, axis=2, keepdims=True)
    weights = jnp.where(allowed, jnp.exp(scores - top), 0.0)
    total = jnp.sum(weights, axis=2, keepdims=True)
    mixed = jnp.einsum(
        "hst,tl->hsl", weights.astype(jnp.bfloat16), new_latent, preferred_element_type=jnp.float32
    )
    mixed = (mixed / total).astype(jnp.bfloat16)
    out = jnp.einsum("hsl,hlv->hsv", mixed, up_value, preferred_element_type=jnp.float32)
    return out, (top + jnp.log(total))[:, :, 0]


def page_lists(page_shard, page_slot, shards):
    kept = page_shard.shape[0]
    rank = jnp.sum(
        (page_shard[:, None] == page_shard[None, :])
        & (jnp.arange(kept)[None, :] < jnp.arange(kept)[:, None]),
        axis=1,
    )
    here = page_shard[None, :] == jnp.arange(shards, dtype=jnp.int32)[:, None]
    counts = jnp.sum(here, axis=1).astype(jnp.int32)
    at = jnp.arange(MAX_PAGES)[None, :, None]
    slots = jnp.sum(
        jnp.where(here[:, None, :] & (rank[None, None, :] == at), page_slot[None, None, :], 0),
        axis=2,
    ).astype(jnp.int32)
    return jnp.concatenate(
        [counts[:, None], slots, jnp.zeros((shards, 15 - MAX_PAGES), jnp.int32)], axis=1
    )


SIDE = 4
HALVES = 2


def corner_index(bits):
    return (bits[0] * 2 + bits[1]) * 2 + bits[2]


def grouped(cores, key):
    groups = {}
    for i in range(SIDE**3):
        at = (i // (SIDE * SIDE), i // SIDE % SIDE, i % SIDE)
        for core in range(cores):
            group, position = key(at, core)
            groups.setdefault((core,) + group, {})[corner_index(position)] = i * cores + core
    return [[group[p] for p in sorted(group)] for _, group in sorted(groups.items())]


def sublattice(at, core):
    return tuple(v % 2 for v in at), tuple(v // 2 for v in at)


def block(at, core):
    return tuple((v - core) % SIDE // 2 for v in at), tuple((v - core) % 2 for v in at)


def exchange(x, key):
    groups = grouped(lax.axis_size("head"), key)
    return lax.all_to_all(
        x, ("batch", "head"), split_axis=0, concat_axis=0, tiled=True, axis_index_groups=groups
    )


def repeat(x):
    return jnp.broadcast_to(x[None], (8,) + x.shape)


def block_position():
    i, core = lax.axis_index("batch"), lax.axis_index("head")
    at = (i // (SIDE * SIDE), i // SIDE % SIDE, i % SIDE)
    return corner_index([(v + SIDE - core) % 2 for v in at]).astype(jnp.int32)


def mix(parts, queries, fresh=None):
    count, rows, _, value = parts.shape
    extra = queries // value
    lse = parts[:, :, queries : queries + 3 * extra].astype(jnp.float32)
    lse = jnp.sum(lse.reshape(count, rows, 3, queries), axis=2)
    top = jnp.max(lse, axis=0)
    if fresh is not None:
        top = jnp.maximum(top, fresh[1])
    share = jnp.exp(lse - top)
    total = jnp.sum(share, axis=0)
    if fresh is not None:
        fresh_share = jnp.exp(fresh[1] - top)
        total = total + fresh_share
    out = jnp.sum(
        parts[:, :, :queries].astype(jnp.float32) * (share / total)[..., None], axis=0
    )
    if fresh is not None:
        out = out + fresh[0] * (fresh_share / total)[..., None]
    return out, top + jnp.log(total)


def pack(out, lse):
    rows, queries, value = out.shape
    pieces, left = [], lse
    for _ in range(3):
        piece = lax.reduce_precision(left, 8, 7)
        left = left - piece
        pieces.append(piece.reshape(rows, queries // value, value))
    extra = 16 - 3 * queries // value
    pieces.append(jnp.zeros((rows, extra, value), jnp.float32))
    return jnp.concatenate([out] + pieces, axis=1).astype(jnp.bfloat16)


def per_device(
    q_nope, q_rope, up_key, up_value, pool_latent, pool_rope,
    new_latent, new_rope, page_shard, page_slot
):
    shards = lax.axis_size("batch")
    steps = q_nope.shape[0]
    heads, nope, latent = up_key.shape
    value = up_value.shape[2]
    slots_total, page, _ = pool_latent.shape
    rope = pool_rope.shape[1] // page
    scale = 1.0 / math.sqrt(nope + rope)
    q_nope = q_nope.reshape(steps, heads, nope)
    q_rope = q_rope.reshape(steps, heads, rope)

    nope_rows = q_nope.transpose(1, 0, 2).reshape(heads * steps, nope)
    rope_rows = q_rope.transpose(1, 0, 2).reshape(2, heads * steps // 2, rope)
    rope_rows = rope_rows.transpose(1, 0, 2).reshape(heads * steps // 2, 2 * rope)
    lists = page_lists(page_shard[0, :, 0], page_slot[0], shards)
    wide = lists.shape[1]
    list_rows = lists.astype(jnp.bfloat16).reshape(shards * wide // nope, nope)
    list_rows = jnp.pad(list_rows, ((0, 16 - list_rows.shape[0]), (0, 0)))
    own = jnp.concatenate([nope_rows, rope_rows, list_rows], axis=0)
    queries = heads * steps
    length = queries + queries // 2

    near = exchange(repeat(own), sublattice)
    count = 8 // HALVES
    pool_rope = pool_rope.reshape(slots_total, page, rope)
    pool_rope = jnp.pad(pool_rope, ((0, 0), (0, 0), (0, 128 - rope)))
    fresh = fresh_part(
        q_nope, q_rope, up_key, up_value, new_latent[:, 0], new_rope.reshape(steps, rope), scale
    )
    near, pool_rope, fresh = lax.optimization_barrier((near, pool_rope, fresh))
    me = lax.axis_index("batch")

    def attend_rows(packed, skip):
        at_row = length + me // (nope // wide)
        lists = lax.dynamic_index_in_dim(packed, at_row, 1, keepdims=False).astype(jnp.int32)
        place = jnp.stack([jnp.int32(skip), me % (nope // wide) * wide]).astype(jnp.int32)
        return attention(lists, place, packed, up_key, up_value, pool_latent, pool_rope, scale)

    position = block_position()
    halves = [near[k * count : (k + 1) * count] for k in range(HALVES)]
    gathered = [exchange(repeat(halves[0]), block), repeat(halves[1])]
    beside = attend_rows(near, -1)
    *gathered, beside = lax.optimization_barrier((*gathered, beside))
    gathered[1] = exchange(gathered[1], block)
    returned = []
    for k in range(HALVES):
        parts = attend_rows(gathered[k].reshape(8 * count, own.shape[0], nope), position)
        if k + 1 < HALVES:
            parts, gathered[k + 1] = lax.optimization_barrier((parts, gathered[k + 1]))
        else:
            parts, returned[0] = lax.optimization_barrier((parts, returned[0]))
        parts = exchange(parts.reshape(8, count, queries + 16, value), block)
        parts = lax.dynamic_update_slice_in_dim(
            parts, beside[None, k * count : (k + 1) * count], position, 0
        )
        returned.append(parts)
    mixed = pack(*mix(returned[0], queries))
    mixed, second = lax.optimization_barrier((mixed, returned[1]))
    rows = jnp.concatenate([mixed, pack(*mix(second, queries))], axis=0)
    rows = exchange(rows, sublattice)
    fresh = (fresh[0].reshape(1, queries, value), fresh[1].reshape(1, queries))
    out, _ = mix(rows[:, None], queries, fresh)
    out = lax.optimization_barrier(out.astype(jnp.bfloat16))
    out = out.reshape(heads, steps, value).transpose(1, 0, 2)
    return out.reshape(steps, 1, heads * value)


def solution(mesh):
    placed = (
        P(None, "batch", "head"),
        P(None, "batch", "head"),
        P("head", None, None),
        P("head", None, None),
        P("batch", None, None),
        P("batch", None),
        P(None, "batch", None),
        P("batch", None),
        P("batch", None, None),
        P("batch", None),
    )
    return jax.shard_map(
        per_device, mesh=mesh, in_specs=placed, out_specs=P(None, "batch", "head"), check_vma=False
    )
```

```python
import functools
import math

import jax
import jax.numpy as jnp
from jax import lax
from jax.experimental import pallas as pl
from jax.experimental.pallas import tpu as pltpu
from jax.sharding import PartitionSpec as P

MAX_PAGES = 10
NEG = -1e30
VMEM_BYTES = 52 * 1024 * 1024
PER = 4
PIECES = 4
NT = (((1,), (1,)), ((), ()))


def sixteen(at):
    return pl.ds(pl.multiple_of(at * 16, 16), 16)

def absorb_step(at, packed, up_ref, held):
    rows, _, nope = packed.shape
    latent = up_ref.shape[2]
    q = packed[:, sixteen(at), :].astype(jnp.float32).reshape(rows, 2, 8, nope)
    first = lax.broadcasted_iota(jnp.int32, (rows, 8, nope), 1) < 4
    halves = []
    for pair in range(2):
        part = q[:, pair]
        wide = jnp.concatenate([jnp.where(first, part, 0.0), jnp.where(first, 0.0, part)], axis=2)
        wide = wide.reshape(rows * 8, 2 * nope).astype(jnp.bfloat16)
        weight = up_ref[pl.ds(at * 4 + 2 * pair, 2)].reshape(2 * nope, latent)
        out = jnp.dot(wide, weight, preferred_element_type=jnp.float32)
        halves.append(out.reshape(rows, 8, latent))
    held[:, sixteen(at), :] = jnp.concatenate(halves, axis=1).astype(jnp.bfloat16)

def project_step(at, held, up_ref, packed):
    rows, _, latent = held.shape
    value = up_ref.shape[2]
    mixed = held[:, sixteen(at), :].astype(jnp.float32).reshape(rows, 2, 8, latent)
    first = lax.broadcasted_iota(jnp.int32, (rows, 8, value), 1) < 4
    halves = []
    for pair in range(2):
        part = mixed[:, pair].reshape(rows * 8, latent).astype(jnp.bfloat16)
        at_head = at * 4 + 2 * pair
        weight = jnp.concatenate([up_ref[at_head], up_ref[at_head + 1]], axis=1)
        out = jnp.dot(part, weight, preferred_element_type=jnp.float32)
        out = out.reshape(rows, 8, 2 * value)
        halves.append(jnp.where(first, out[:, :, :value], out[:, :, value:]))
    packed[:, sixteen(at), :] = jnp.concatenate(halves, axis=1).astype(jnp.bfloat16)

def attend_step(scale, at, lists_ref, shift, packed_ref, lat_ref, keyrope_ref, held, keys, rotated, tops, totals):
    queries, latent = held.shape[1:]
    page = lat_ref.shape[1]
    counts = [lists_ref[at * PER + i, shift] for i in range(PER)]
    most = functools.reduce(jnp.maximum, counts)

    def run(pages):
        tokens = pages * page
        lanes = lax.broadcasted_iota(jnp.int32, (queries, 128), 1)
        token = lax.broadcasted_iota(jnp.int32, (1, tokens), 1)
        all_scores = []
        for i in range(PER):
            r = at * PER + i
            for k in range(pages):
                slot = lists_ref[r, shift + 1 + k]
                keys[i, k * page : (k + 1) * page, :] = lat_ref[slot]
                rotated[i, k * page : (k + 1) * page, :] = keyrope_ref[slot]
            packed = packed_ref[r, queries : queries + queries // 2, :]
            half = packed.shape[1] // 2
            q_rope = jnp.concatenate([packed[:, :half], packed[:, half:]], axis=0)
            bias = jnp.where(token < counts[i] * page, 0.0, NEG)
            scores = lax.dot_general(held[r], keys[i, 0:tokens, :], NT, preferred_element_type=jnp.float32)
            scores += lax.dot_general(q_rope, rotated[i, 0:tokens, :half], NT, preferred_element_type=jnp.float32)
            all_scores.append(scores + bias)
        for i in range(PER):
            r = at * PER + i
            scores = all_scores[i]
            top = jnp.max(scores, axis=1, keepdims=True)
            weights = jnp.exp2((scores - top) * (scale * math.log2(math.e)))
            total = jnp.sum(weights, axis=1, keepdims=True)
            mixed = jnp.dot(weights.astype(jnp.bfloat16), keys[i, 0:tokens, :], preferred_element_type=jnp.float32)
            held[r] = (mixed * (1.0 / total)).astype(jnp.bfloat16)
            tops[...] = jnp.where(lanes == r, top, tops[...])
            totals[...] = jnp.where(lanes == r, total, totals[...])

    pl.when(most <= 4)(lambda: run(4))
    pl.when((most > 4) & (most <= 6))(lambda: run(6))
    pl.when((most > 6) & (most <= 8))(lambda: run(8))
    pl.when(most > 8)(lambda: run(10))

def share_step(scale, tops, totals, packed):
    rows, _, width = packed.shape
    queries = tops.shape[0]
    lse = tops[...] * scale + jnp.log(jnp.maximum(totals[...], 1e-30))
    lse = lse.T[:rows]
    row = lax.broadcasted_iota(jnp.int32, (rows, 8, width), 1)
    out = jnp.zeros((rows, 8, width), jnp.float32)
    left = lse
    per = queries // width
    for level in range(3):
        piece = left.astype(jnp.bfloat16).astype(jnp.float32)
        left = left - piece
        for c in range(per):
            part = piece[:, c * width : (c + 1) * width].reshape(rows, 1, width)
            out = jnp.where(row == level * per + c, part, out)
    packed[:, queries : queries + 16, :] = jnp.concatenate([out, jnp.zeros_like(out)], axis=1).astype(jnp.bfloat16)

def body(scale, repeats, lists_ref, place_ref, packed_hbm, upk_hbm, lat_hbm, keyrope_hbm, upv_hbm, out_hbm,
         *refs):
    repeated = None
    if repeats:
        repeated, *refs = refs
    packed, upk, lat, keyrope, upv, held, keys, rotated, tops, totals, *sems = refs
    in_sems, key_sems, value_sems, out_sems, repeat_sems = sems
    heads = upk.shape[0]
    queries = held.shape[1]
    groups = heads // 4
    chunk = heads // PIECES

    def piece(hbm, vmem, sems, k):
        span = pl.ds(k * chunk, chunk)
        return pltpu.make_async_copy(hbm.at[span], vmem.at[span], sems.at[k])

    def repeat_copy(k):
        half = packed_hbm.shape[0] // 2
        return pltpu.make_async_copy(
            packed_hbm.at[pl.ds(half, half)], repeated.at[k], repeat_sems.at[k]
        )

    def out_copy(at):
        return pltpu.make_async_copy(packed.at[:, sixteen(at), :], out_hbm.at[:, sixteen(at), :], out_sems.at[at])

    load_packed = pltpu.make_async_copy(
        packed_hbm.at[:, pl.ds(0, packed.shape[1]), :], packed, in_sems.at[0]
    )
    load_lat = pltpu.make_async_copy(lat_hbm, lat, in_sems.at[1])
    load_rope = pltpu.make_async_copy(keyrope_hbm, keyrope, in_sems.at[2])
    load_packed.start()
    for k in range(PIECES):
        piece(upk_hbm, upk, key_sems, k).start()
    load_lat.start()
    load_rope.start()
    tops[...] = jnp.zeros_like(tops)
    totals[...] = jnp.ones_like(totals)
    load_packed.wait()

    def absorb(k, _):
        piece(upk_hbm, upk, key_sems, k).wait()
        for j in range(groups // PIECES):
            absorb_step(k * (groups // PIECES) + j, packed, upk, held)
        return 0

    lax.fori_loop(0, PIECES, absorb, 0)

    load_lat.wait()
    load_rope.wait()
    for k in range(PIECES):
        piece(upv_hbm, upv, value_sems, k).start()
    for k in range(repeats):
        repeat_copy(k).start()

    def attend(at, _):
        @pl.when(at != place_ref[0])
        def _():
            attend_step(
                scale, at, lists_ref, place_ref[1], packed, lat, keyrope, held, keys, rotated, tops, totals
            )
        return 0

    lax.fori_loop(0, held.shape[0] // PER, attend, 0)

    share_step(scale, tops, totals, packed)
    out_copy(groups).start()
    def project(k, _):
        piece(upv_hbm, upv, value_sems, k).wait()
        for j in range(groups // PIECES):
            at = k * (groups // PIECES) + j
            project_step(at, held, upv, packed)
            out_copy(at).start()
        return 0

    lax.fori_loop(0, PIECES, project, 0)

    def drain(at, _):
        out_copy(at).wait()
        return 0
    lax.fori_loop(0, groups + 1, drain, 0)
    for k in range(repeats):
        repeat_copy(k).wait()

def attention(lists, place, packed, up_key, up_value, pool_latent, pool_rope, scale, repeats=0):
    rows = packed.shape[0]
    heads, nope, latent = up_key.shape
    value = up_value.shape[2]
    queries = heads * 4
    page = pool_latent.shape[1]
    rope = pool_rope.shape[2]
    anywhere = pl.BlockSpec(memory_space=pl.ANY)
    outs = [jax.ShapeDtypeStruct((rows, queries + 16, value), jnp.bfloat16)]
    if repeats:
        outs.append(jax.ShapeDtypeStruct((repeats, rows // 2) + packed.shape[1:], jnp.bfloat16))
    scalars = pl.BlockSpec(memory_space=pltpu.SMEM)
    return pl.pallas_call(
        functools.partial(body, scale, repeats),
        out_shape=outs if repeats else outs[0],
        in_specs=[scalars] * 2 + [anywhere] * 5,
        out_specs=[anywhere] * len(outs) if repeats else anywhere,
        scratch_shapes=[
            pltpu.VMEM((rows, queries + queries // 2, nope), jnp.bfloat16),
            pltpu.VMEM(up_key.shape, jnp.bfloat16),
            pltpu.VMEM(pool_latent.shape, jnp.bfloat16),
            pltpu.VMEM(pool_rope.shape, jnp.bfloat16),
            pltpu.VMEM(up_value.shape, jnp.bfloat16),
            pltpu.VMEM((rows, queries, latent), jnp.bfloat16),
            pltpu.VMEM((PER, MAX_PAGES * page, latent), jnp.bfloat16),
            pltpu.VMEM((PER, MAX_PAGES * page, rope), jnp.bfloat16),
            pltpu.VMEM((queries, 128), jnp.float32),
            pltpu.VMEM((queries, 128), jnp.float32),
            pltpu.SemaphoreType.DMA((3,)),
            pltpu.SemaphoreType.DMA((PIECES,)),
            pltpu.SemaphoreType.DMA((PIECES,)),
            pltpu.SemaphoreType.DMA((heads // 4 + 1,)),
            pltpu.SemaphoreType.DMA((8,)),
        ],
        compiler_params=pltpu.CompilerParams(vmem_limit_bytes=VMEM_BYTES),
        cost_estimate=pl.CostEstimate(
            flops=rows * queries * 640 * 4 * latent, bytes_accessed=1 << 27, transcendentals=0
        ),
        name="attention",
    )(lists, place, packed, up_key, pool_latent, pool_rope, up_value)


def fresh_part(q_nope, q_rope, up_key, up_value, new_latent, new_rope, scale):
    steps, heads, _ = q_nope.shape
    latent = up_key.shape[2]
    absorbed = jnp.einsum(
        "shn,hnl->hsl", q_nope, up_key, preferred_element_type=jnp.float32
    ).astype(jnp.bfloat16)
    scores = (
        jnp.einsum("hsl,tl->hst", absorbed, new_latent, preferred_element_type=jnp.float32)
        + jnp.einsum("she,te->hst", q_rope, new_rope, preferred_element_type=jnp.float32)
    ) * scale
    at = jnp.arange(steps, dtype=jnp.int32)
    allowed = at[None, None, :] <= at[None, :, None]
    scores = jnp.where(allowed, scores, NEG)
    top = jnp.max(scores, axis=2, keepdims=True)
    weights = jnp.where(allowed, jnp.exp(scores - top), 0.0)
    total = jnp.sum(weights, axis=2, keepdims=True)
    mixed = jnp.einsum(
        "hst,tl->hsl", weights.astype(jnp.bfloat16), new_latent, preferred_element_type=jnp.float32
    )
    mixed = (mixed / total).astype(jnp.bfloat16)
    out = jnp.einsum("hsl,hlv->hsv", mixed, up_value, preferred_element_type=jnp.float32)
    return out, (top + jnp.log(total))[:, :, 0]


def page_lists(page_shard, page_slot, shards):
    kept = page_shard.shape[0]
    rank = jnp.sum(
        (page_shard[:, None] == page_shard[None, :])
        & (jnp.arange(kept)[None, :] < jnp.arange(kept)[:, None]),
        axis=1,
    )
    here = page_shard[None, :] == jnp.arange(shards, dtype=jnp.int32)[:, None]
    counts = jnp.sum(here, axis=1).astype(jnp.int32)
    at = jnp.arange(MAX_PAGES)[None, :, None]
    slots = jnp.sum(
        jnp.where(here[:, None, :] & (rank[None, None, :] == at), page_slot[None, None, :], 0),
        axis=2,
    ).astype(jnp.int32)
    return jnp.concatenate(
        [counts[:, None], slots, jnp.zeros((shards, 15 - MAX_PAGES), jnp.int32)], axis=1
    )


SIDE = 4
HALVES = 2


def corner_index(bits):
    return (bits[0] * 2 + bits[1]) * 2 + bits[2]


def grouped(cores, key):
    groups = {}
    for i in range(SIDE**3):
        at = (i // (SIDE * SIDE), i // SIDE % SIDE, i % SIDE)
        for core in range(cores):
            group, position = key(at, core)
            groups.setdefault((core,) + group, {})[corner_index(position)] = i * cores + core
    return [[group[p] for p in sorted(group)] for _, group in sorted(groups.items())]


def sublattice(at, core):
    return tuple(v % 2 for v in at), tuple(v // 2 for v in at)


def block(at, core):
    return tuple((v - core) % SIDE // 2 for v in at), tuple((v - core) % 2 for v in at)


def exchange(x, key):
    groups = grouped(lax.axis_size("head"), key)
    return lax.all_to_all(
        x, ("batch", "head"), split_axis=0, concat_axis=0, tiled=True, axis_index_groups=groups
    )


def repeat(x):
    return jnp.broadcast_to(x[None], (8,) + x.shape)


def block_position():
    i, core = lax.axis_index("batch"), lax.axis_index("head")
    at = (i // (SIDE * SIDE), i // SIDE % SIDE, i % SIDE)
    return corner_index([(v + SIDE - core) % 2 for v in at]).astype(jnp.int32)


def mix(parts, queries, fresh=None):
    count, rows, _, value = parts.shape
    extra = queries // value
    lse = parts[:, :, queries : queries + 3 * extra].astype(jnp.float32)
    lse = jnp.sum(lse.reshape(count, rows, 3, queries), axis=2)
    top = jnp.max(lse, axis=0)
    if fresh is not None:
        top = jnp.maximum(top, fresh[1])
    share = jnp.exp(lse - top)
    total = jnp.sum(share, axis=0)
    if fresh is not None:
        fresh_share = jnp.exp(fresh[1] - top)
        total = total + fresh_share
    out = jnp.sum(
        parts[:, :, :queries].astype(jnp.float32) * (share / total)[..., None], axis=0
    )
    if fresh is not None:
        out = out + fresh[0] * (fresh_share / total)[..., None]
    return out, top + jnp.log(total)


def pack(out, lse):
    rows, queries, value = out.shape
    pieces, left = [], lse
    for _ in range(3):
        piece = lax.reduce_precision(left, 8, 7)
        left = left - piece
        pieces.append(piece.reshape(rows, queries // value, value))
    extra = 16 - 3 * queries // value
    pieces.append(jnp.zeros((rows, extra, value), jnp.float32))
    return jnp.concatenate([out] + pieces, axis=1).astype(jnp.bfloat16)


def per_device(
    q_nope, q_rope, up_key, up_value, pool_latent, pool_rope,
    new_latent, new_rope, page_shard, page_slot
):
    shards = lax.axis_size("batch")
    steps = q_nope.shape[0]
    heads, nope, latent = up_key.shape
    value = up_value.shape[2]
    slots_total, page, _ = pool_latent.shape
    rope = pool_rope.shape[1] // page
    scale = 1.0 / math.sqrt(nope + rope)
    q_nope = q_nope.reshape(steps, heads, nope)
    q_rope = q_rope.reshape(steps, heads, rope)

    nope_rows = q_nope.transpose(1, 0, 2).reshape(heads * steps, nope)
    rope_rows = q_rope.transpose(1, 0, 2).reshape(2, heads * steps // 2, rope)
    rope_rows = rope_rows.transpose(1, 0, 2).reshape(heads * steps // 2, 2 * rope)
    lists = page_lists(page_shard[0, :, 0], page_slot[0], shards)
    wide = lists.shape[1]
    list_rows = lists.astype(jnp.bfloat16).reshape(shards * wide // nope, nope)
    list_rows = jnp.pad(list_rows, ((0, 16 - list_rows.shape[0]), (0, 0)))
    own = jnp.concatenate([nope_rows, rope_rows, list_rows], axis=0)
    queries = heads * steps
    length = queries + queries // 2

    near = exchange(repeat(own), sublattice)
    count = 8 // HALVES
    pool_rope = pool_rope.reshape(slots_total, page, rope)
    pool_rope = jnp.pad(pool_rope, ((0, 0), (0, 0), (0, 128 - rope)))
    fresh = fresh_part(
        q_nope, q_rope, up_key, up_value, new_latent[:, 0], new_rope.reshape(steps, rope), scale
    )
    near, pool_rope, fresh = lax.optimization_barrier((near, pool_rope, fresh))
    me = lax.axis_index("batch")

    def attend_rows(packed, skip, repeats=0):
        at_row = length + me // (nope // wide)
        lists = lax.dynamic_index_in_dim(packed, at_row, 1, keepdims=False).astype(jnp.int32)
        place = jnp.stack([jnp.int32(skip), me % (nope // wide) * wide]).astype(jnp.int32)
        return attention(
            lists, place, packed, up_key, up_value, pool_latent, pool_rope, scale, repeats
        )

    position = block_position()
    first = exchange(repeat(near[:count]), block)
    beside, second = attend_rows(near, -1, 8)
    first, second, beside = lax.optimization_barrier((first, second, beside))
    gathered = [first, second]
    gathered[1] = exchange(gathered[1], block)
    returned = []
    for k in range(HALVES):
        parts = attend_rows(gathered[k].reshape(8 * count, own.shape[0], nope), position)
        if k + 1 < HALVES:
            parts, gathered[k + 1] = lax.optimization_barrier((parts, gathered[k + 1]))
        else:
            parts, returned[0] = lax.optimization_barrier((parts, returned[0]))
        parts = exchange(parts.reshape(8, count, queries + 16, value), block)
        parts = lax.dynamic_update_slice_in_dim(
            parts, beside[None, k * count : (k + 1) * count], position, 0
        )
        returned.append(parts)
    mixed = pack(*mix(returned[0], queries))
    mixed, second = lax.optimization_barrier((mixed, returned[1]))
    rows = jnp.concatenate([mixed, pack(*mix(second, queries))], axis=0)
    rows = exchange(rows, sublattice)
    fresh = (fresh[0].reshape(1, queries, value), fresh[1].reshape(1, queries))
    out, _ = mix(rows[:, None], queries, fresh)
    out = lax.optimization_barrier(out.astype(jnp.bfloat16))
    out = out.reshape(heads, steps, value).transpose(1, 0, 2)
    return out.reshape(steps, 1, heads * value)


def solution(mesh):
    placed = (
        P(None, "batch", "head"),
        P(None, "batch", "head"),
        P("head", None, None),
        P("head", None, None),
        P("batch", None, None),
        P("batch", None),
        P(None, "batch", None),
        P("batch", None),
        P("batch", None, None),
        P("batch", None),
    )
    return jax.shard_map(
        per_device, mesh=mesh, in_specs=placed, out_specs=P(None, "batch", "head"), check_vma=False
    )
```

```python
import functools
import math

import jax
import jax.numpy as jnp
from jax import lax
from jax.experimental import pallas as pl
from jax.experimental.pallas import tpu as pltpu
from jax.sharding import PartitionSpec as P

MAX_PAGES = 10
NEG = -1e30
VMEM_BYTES = 52 * 1024 * 1024
PER = 4
PIECES = 4
NT = (((1,), (1,)), ((), ()))


def sixteen(at):
    return pl.ds(pl.multiple_of(at * 16, 16), 16)

def absorb_step(at, packed, up_ref, held):
    rows, _, nope = packed.shape
    latent = up_ref.shape[2]
    q = packed[:, sixteen(at), :].astype(jnp.float32).reshape(rows, 2, 8, nope)
    first = lax.broadcasted_iota(jnp.int32, (rows, 8, nope), 1) < 4
    halves = []
    for pair in range(2):
        part = q[:, pair]
        wide = jnp.concatenate([jnp.where(first, part, 0.0), jnp.where(first, 0.0, part)], axis=2)
        wide = wide.reshape(rows * 8, 2 * nope).astype(jnp.bfloat16)
        weight = up_ref[pl.ds(at * 4 + 2 * pair, 2)].reshape(2 * nope, latent)
        out = jnp.dot(wide, weight, preferred_element_type=jnp.float32)
        halves.append(out.reshape(rows, 8, latent))
    held[:, sixteen(at), :] = jnp.concatenate(halves, axis=1).astype(jnp.bfloat16)

def project_step(at, held, up_ref, packed):
    rows, _, latent = held.shape
    value = up_ref.shape[2]
    mixed = held[:, sixteen(at), :].astype(jnp.float32).reshape(rows, 2, 8, latent)
    first = lax.broadcasted_iota(jnp.int32, (rows, 8, value), 1) < 4
    halves = []
    for pair in range(2):
        part = mixed[:, pair].reshape(rows * 8, latent).astype(jnp.bfloat16)
        at_head = at * 4 + 2 * pair
        weight = jnp.concatenate([up_ref[at_head], up_ref[at_head + 1]], axis=1)
        out = jnp.dot(part, weight, preferred_element_type=jnp.float32)
        out = out.reshape(rows, 8, 2 * value)
        halves.append(jnp.where(first, out[:, :, :value], out[:, :, value:]))
    packed[:, sixteen(at), :] = jnp.concatenate(halves, axis=1).astype(jnp.bfloat16)

def attend_step(scale, at, lists_ref, shift, packed_ref, lat_ref, keyrope_ref, held, keys, rotated, tops, totals):
    queries, latent = held.shape[1:]
    page = lat_ref.shape[1]
    counts = [lists_ref[at * PER + i, shift] for i in range(PER)]
    most = functools.reduce(jnp.maximum, counts)

    def run(pages):
        tokens = pages * page
        lanes = lax.broadcasted_iota(jnp.int32, (queries, 128), 1)
        token = lax.broadcasted_iota(jnp.int32, (1, tokens), 1)
        all_scores = []
        for i in range(PER):
            r = at * PER + i
            for k in range(pages):
                slot = lists_ref[r, shift + 1 + k]
                keys[i, k * page : (k + 1) * page, :] = lat_ref[slot]
                rotated[i, k * page : (k + 1) * page, :] = keyrope_ref[slot]
            packed = packed_ref[r, queries : queries + queries // 2, :]
            half = packed.shape[1] // 2
            q_rope = jnp.concatenate([packed[:, :half], packed[:, half:]], axis=0)
            bias = jnp.where(token < counts[i] * page, 0.0, NEG)
            scores = lax.dot_general(held[r], keys[i, 0:tokens, :], NT, preferred_element_type=jnp.float32)
            scores += lax.dot_general(q_rope, rotated[i, 0:tokens, :half], NT, preferred_element_type=jnp.float32)
            all_scores.append(scores + bias)
        for i in range(PER):
            r = at * PER + i
            scores = all_scores[i]
            top = jnp.max(scores, axis=1, keepdims=True)
            weights = jnp.exp2((scores - top) * (scale * math.log2(math.e)))
            total = jnp.sum(weights, axis=1, keepdims=True)
            mixed = jnp.dot(weights.astype(jnp.bfloat16), keys[i, 0:tokens, :], preferred_element_type=jnp.float32)
            held[r] = (mixed * (1.0 / total)).astype(jnp.bfloat16)
            tops[...] = jnp.where(lanes == r, top, tops[...])
            totals[...] = jnp.where(lanes == r, total, totals[...])

    pl.when(most <= 4)(lambda: run(4))
    pl.when((most > 4) & (most <= 6))(lambda: run(6))
    pl.when((most > 6) & (most <= 8))(lambda: run(8))
    pl.when(most > 8)(lambda: run(10))

def share_step(scale, tops, totals, packed):
    rows, _, width = packed.shape
    queries = tops.shape[0]
    lse = tops[...] * scale + jnp.log(jnp.maximum(totals[...], 1e-30))
    lse = lse.T[:rows]
    row = lax.broadcasted_iota(jnp.int32, (rows, 8, width), 1)
    out = jnp.zeros((rows, 8, width), jnp.float32)
    left = lse
    per = queries // width
    for level in range(3):
        piece = left.astype(jnp.bfloat16).astype(jnp.float32)
        left = left - piece
        for c in range(per):
            part = piece[:, c * width : (c + 1) * width].reshape(rows, 1, width)
            out = jnp.where(row == level * per + c, part, out)
    packed[:, queries : queries + 16, :] = jnp.concatenate([out, jnp.zeros_like(out)], axis=1).astype(jnp.bfloat16)

def body(scale, repeats, lists_ref, place_ref, packed_hbm, upk_hbm, lat_hbm, keyrope_hbm, upv_hbm, out_hbm,
         *refs):
    repeated = None
    if repeats:
        repeated, *refs = refs
    packed, upk, lat, keyrope, upv, held, keys, rotated, tops, totals, *sems = refs
    in_sems, key_sems, value_sems, out_sems, repeat_sems = sems
    heads = upk.shape[0]
    queries = held.shape[1]
    groups = heads // 4
    chunk = heads // PIECES

    def piece(hbm, vmem, sems, k):
        span = pl.ds(k * chunk, chunk)
        return pltpu.make_async_copy(hbm.at[span], vmem.at[span], sems.at[k])

    def repeat_copy(k):
        half = packed_hbm.shape[0] // 2
        return pltpu.make_async_copy(
            packed_hbm.at[pl.ds(half, half)], repeated.at[k], repeat_sems.at[k]
        )

    def out_copy(at):
        return pltpu.make_async_copy(packed.at[:, sixteen(at), :], out_hbm.at[:, sixteen(at), :], out_sems.at[at])

    load_packed = pltpu.make_async_copy(
        packed_hbm.at[:, pl.ds(0, packed.shape[1]), :], packed, in_sems.at[0]
    )
    load_lat = pltpu.make_async_copy(lat_hbm, lat, in_sems.at[1])
    load_rope = pltpu.make_async_copy(keyrope_hbm, keyrope, in_sems.at[2])
    load_packed.start()
    for k in range(PIECES):
        piece(upk_hbm, upk, key_sems, k).start()
    load_lat.start()
    load_rope.start()
    tops[...] = jnp.zeros_like(tops)
    totals[...] = jnp.ones_like(totals)
    load_packed.wait()

    def absorb(k, _):
        piece(upk_hbm, upk, key_sems, k).wait()
        for j in range(groups // PIECES):
            absorb_step(k * (groups // PIECES) + j, packed, upk, held)
        return 0

    lax.fori_loop(0, PIECES, absorb, 0)

    load_lat.wait()
    load_rope.wait()
    for k in range(PIECES):
        piece(upv_hbm, upv, value_sems, k).start()
    for k in range(repeats):
        repeat_copy(k).start()

    def attend(at, _):
        @pl.when(at != place_ref[0])
        def _():
            attend_step(
                scale, at, lists_ref, place_ref[1], packed, lat, keyrope, held, keys, rotated, tops, totals
            )
        return 0

    lax.fori_loop(0, held.shape[0] // PER, attend, 0)

    share_step(scale, tops, totals, packed)
    out_copy(groups).start()
    def project(k, _):
        piece(upv_hbm, upv, value_sems, k).wait()
        for j in range(groups // PIECES):
            at = k * (groups // PIECES) + j
            project_step(at, held, upv, packed)
            out_copy(at).start()
        return 0

    lax.fori_loop(0, PIECES, project, 0)

    def drain(at, _):
        out_copy(at).wait()
        return 0
    lax.fori_loop(0, groups + 1, drain, 0)
    for k in range(repeats):
        repeat_copy(k).wait()

def attention(lists, place, packed, up_key, up_value, pool_latent, pool_rope, scale, repeats=0):
    rows = packed.shape[0]
    heads, nope, latent = up_key.shape
    value = up_value.shape[2]
    queries = heads * 4
    page = pool_latent.shape[1]
    rope = pool_rope.shape[2]
    anywhere = pl.BlockSpec(memory_space=pl.ANY)
    outs = [jax.ShapeDtypeStruct((rows, queries + 16, value), jnp.bfloat16)]
    if repeats:
        outs.append(jax.ShapeDtypeStruct((repeats, rows // 2) + packed.shape[1:], jnp.bfloat16))
    scalars = pl.BlockSpec(memory_space=pltpu.SMEM)
    return pl.pallas_call(
        functools.partial(body, scale, repeats),
        out_shape=outs if repeats else outs[0],
        in_specs=[scalars] * 2 + [anywhere] * 5,
        out_specs=[anywhere] * len(outs) if repeats else anywhere,
        scratch_shapes=[
            pltpu.VMEM((rows, queries + queries // 2, nope), jnp.bfloat16),
            pltpu.VMEM(up_key.shape, jnp.bfloat16),
            pltpu.VMEM(pool_latent.shape, jnp.bfloat16),
            pltpu.VMEM(pool_rope.shape, jnp.bfloat16),
            pltpu.VMEM(up_value.shape, jnp.bfloat16),
            pltpu.VMEM((rows, queries, latent), jnp.bfloat16),
            pltpu.VMEM((PER, MAX_PAGES * page, latent), jnp.bfloat16),
            pltpu.VMEM((PER, MAX_PAGES * page, rope), jnp.bfloat16),
            pltpu.VMEM((queries, 128), jnp.float32),
            pltpu.VMEM((queries, 128), jnp.float32),
            pltpu.SemaphoreType.DMA((3,)),
            pltpu.SemaphoreType.DMA((PIECES,)),
            pltpu.SemaphoreType.DMA((PIECES,)),
            pltpu.SemaphoreType.DMA((heads // 4 + 1,)),
            pltpu.SemaphoreType.DMA((8,)),
        ],
        compiler_params=pltpu.CompilerParams(vmem_limit_bytes=VMEM_BYTES),
        cost_estimate=pl.CostEstimate(
            flops=rows * queries * 640 * 4 * latent, bytes_accessed=1 << 27, transcendentals=0
        ),
        name="attention",
    )(lists, place, packed, up_key, pool_latent, pool_rope, up_value)


def fresh_part(q_nope, q_rope, up_key, up_value, new_latent, new_rope, scale):
    steps, heads, _ = q_nope.shape
    latent = up_key.shape[2]
    absorbed = jnp.einsum(
        "shn,hnl->hsl", q_nope, up_key, preferred_element_type=jnp.float32
    ).astype(jnp.bfloat16)
    scores = (
        jnp.einsum("hsl,tl->hst", absorbed, new_latent, preferred_element_type=jnp.float32)
        + jnp.einsum("she,te->hst", q_rope, new_rope, preferred_element_type=jnp.float32)
    ) * scale
    at = jnp.arange(steps, dtype=jnp.int32)
    allowed = at[None, None, :] <= at[None, :, None]
    scores = jnp.where(allowed, scores, NEG)
    top = jnp.max(scores, axis=2, keepdims=True)
    weights = jnp.where(allowed, jnp.exp(scores - top), 0.0)
    total = jnp.sum(weights, axis=2, keepdims=True)
    mixed = jnp.einsum(
        "hst,tl->hsl", weights.astype(jnp.bfloat16), new_latent, preferred_element_type=jnp.float32
    )
    mixed = (mixed / total).astype(jnp.bfloat16)
    out = jnp.einsum("hsl,hlv->hsv", mixed, up_value, preferred_element_type=jnp.float32)
    return out, (top + jnp.log(total))[:, :, 0]


def page_lists(page_shard, page_slot, shards):
    kept = page_shard.shape[0]
    rank = jnp.sum(
        (page_shard[:, None] == page_shard[None, :])
        & (jnp.arange(kept)[None, :] < jnp.arange(kept)[:, None]),
        axis=1,
    )
    here = page_shard[None, :] == jnp.arange(shards, dtype=jnp.int32)[:, None]
    counts = jnp.sum(here, axis=1).astype(jnp.int32)
    at = jnp.arange(MAX_PAGES)[None, :, None]
    slots = jnp.sum(
        jnp.where(here[:, None, :] & (rank[None, None, :] == at), page_slot[None, None, :], 0),
        axis=2,
    ).astype(jnp.int32)
    return jnp.concatenate(
        [counts[:, None], slots, jnp.zeros((shards, 15 - MAX_PAGES), jnp.int32)], axis=1
    )


SIDE = 4
HALVES = 2


def corner_index(bits):
    return (bits[0] * 2 + bits[1]) * 2 + bits[2]


def grouped(cores, key):
    groups = {}
    for i in range(SIDE**3):
        at = (i // (SIDE * SIDE), i // SIDE % SIDE, i % SIDE)
        for core in range(cores):
            group, position = key(at, core)
            groups.setdefault((core,) + group, {})[corner_index(position)] = i * cores + core
    return [[group[p] for p in sorted(group)] for _, group in sorted(groups.items())]


def sublattice(at, core):
    return tuple(v % 2 for v in at), tuple(v // 2 for v in at)


def block(at, core):
    return tuple((v - core) % SIDE // 2 for v in at), tuple((v - core) % 2 for v in at)


def exchange(x, key):
    groups = grouped(lax.axis_size("head"), key)
    return lax.all_to_all(
        x, ("batch", "head"), split_axis=0, concat_axis=0, tiled=True, axis_index_groups=groups
    )


def repeat(x):
    return jnp.broadcast_to(x[None], (8,) + x.shape)


def block_position():
    i, core = lax.axis_index("batch"), lax.axis_index("head")
    at = (i // (SIDE * SIDE), i // SIDE % SIDE, i % SIDE)
    return corner_index([(v + SIDE - core) % 2 for v in at]).astype(jnp.int32)


def mix(parts, queries, fresh=None):
    count, rows, _, value = parts.shape
    extra = queries // value
    lse = parts[:, :, queries : queries + 3 * extra].astype(jnp.float32)
    lse = jnp.sum(lse.reshape(count, rows, 3, queries), axis=2)
    top = jnp.max(lse, axis=0)
    if fresh is not None:
        top = jnp.maximum(top, fresh[1])
    share = jnp.exp(lse - top)
    total = jnp.sum(share, axis=0)
    if fresh is not None:
        fresh_share = jnp.exp(fresh[1] - top)
        total = total + fresh_share
    out = jnp.sum(
        parts[:, :, :queries].astype(jnp.float32) * (share / total)[..., None], axis=0
    )
    if fresh is not None:
        out = out + fresh[0] * (fresh_share / total)[..., None]
    return out, top + jnp.log(total)


def pack(out, lse):
    rows, queries, value = out.shape
    pieces, left = [], lse
    for _ in range(3):
        piece = lax.reduce_precision(left, 8, 7)
        left = left - piece
        pieces.append(piece.reshape(rows, queries // value, value))
    extra = 16 - 3 * queries // value
    pieces.append(jnp.zeros((rows, extra, value), jnp.float32))
    return jnp.concatenate([out] + pieces, axis=1).astype(jnp.bfloat16)


def per_device(
    q_nope, q_rope, up_key, up_value, pool_latent, pool_rope,
    new_latent, new_rope, page_shard, page_slot
):
    shards = lax.axis_size("batch")
    steps = q_nope.shape[0]
    heads, nope, latent = up_key.shape
    value = up_value.shape[2]
    slots_total, page, _ = pool_latent.shape
    rope = pool_rope.shape[1] // page
    scale = 1.0 / math.sqrt(nope + rope)
    q_nope = q_nope.reshape(steps, heads, nope)
    q_rope = q_rope.reshape(steps, heads, rope)

    nope_rows = q_nope.transpose(1, 0, 2).reshape(heads * steps, nope)
    rope_rows = q_rope.transpose(1, 0, 2).reshape(2, heads * steps // 2, rope)
    rope_rows = rope_rows.transpose(1, 0, 2).reshape(heads * steps // 2, 2 * rope)
    lists = page_lists(page_shard[0, :, 0], page_slot[0], shards)
    wide = lists.shape[1]
    list_rows = lists.astype(jnp.bfloat16).reshape(shards * wide // nope, nope)
    list_rows = jnp.pad(list_rows, ((0, 16 - list_rows.shape[0]), (0, 0)))
    own = jnp.concatenate([nope_rows, rope_rows, list_rows], axis=0)
    queries = heads * steps
    length = queries + queries // 2

    near = exchange(repeat(own), sublattice)
    count = 8 // HALVES
    pool_rope = pool_rope.reshape(slots_total, page, rope)
    pool_rope = jnp.pad(pool_rope, ((0, 0), (0, 0), (0, 128 - rope)))
    fresh = fresh_part(
        q_nope, q_rope, up_key, up_value, new_latent[:, 0], new_rope.reshape(steps, rope), scale
    )
    near, pool_rope, fresh = lax.optimization_barrier((near, pool_rope, fresh))
    me = lax.axis_index("batch")

    def attend_rows(packed, skip, repeats=0):
        at_row = length + me // (nope // wide)
        lists = lax.dynamic_index_in_dim(packed, at_row, 1, keepdims=False).astype(jnp.int32)
        place = jnp.stack([jnp.int32(skip), me % (nope // wide) * wide]).astype(jnp.int32)
        return attention(
            lists, place, packed, up_key, up_value, pool_latent, pool_rope, scale, repeats
        )

    position = block_position()
    first = exchange(repeat(near[:count]), block)
    beside, second = attend_rows(near, -1, 8)
    first, second, beside = lax.optimization_barrier((first, second, beside))
    gathered = [first, second]
    gathered[1] = exchange(gathered[1], block)
    returned = []
    for k in range(HALVES):
        parts = attend_rows(gathered[k].reshape(8 * count, own.shape[0], nope), position)
        if k + 1 < HALVES:
            parts, gathered[k + 1] = lax.optimization_barrier((parts, gathered[k + 1]))
        else:
            parts, returned[0] = lax.optimization_barrier((parts, returned[0]))
        parts = exchange(parts.reshape(8, count, queries + 16, value), block)
        returned.append(parts)
    def with_own(parts, k):
        own_part = beside[None, k * count : (k + 1) * count]
        return lax.dynamic_update_slice_in_dim(parts, own_part, position, 0)

    mixed = pack(*mix(with_own(returned[0], 0), queries))
    mixed, second = lax.optimization_barrier((mixed, returned[1]))
    second = with_own(second, 1)
    rows = jnp.concatenate([mixed, pack(*mix(second, queries))], axis=0)
    rows = exchange(rows, sublattice)
    fresh = (fresh[0].reshape(1, queries, value), fresh[1].reshape(1, queries))
    out, _ = mix(rows[:, None], queries, fresh)
    out = lax.optimization_barrier(out.astype(jnp.bfloat16))
    out = out.reshape(heads, steps, value).transpose(1, 0, 2)
    return out.reshape(steps, 1, heads * value)


def solution(mesh):
    placed = (
        P(None, "batch", "head"),
        P(None, "batch", "head"),
        P("head", None, None),
        P("head", None, None),
        P("batch", None, None),
        P("batch", None),
        P(None, "batch", None),
        P("batch", None),
        P("batch", None, None),
        P("batch", None),
    )
    return jax.shard_map(
        per_device, mesh=mesh, in_specs=placed, out_specs=P(None, "batch", "head"), check_vma=False
    )
```
